256 devices in a mesh: ctx: 16 (over x_lo, y, core), head: 16 (over x_hi, z).
Axes of the slice: x: 4 (x_hi: 2, x_lo: 2; x = x_hi * 2 + x_lo), y: 4, z: 8, core: 2. Of those that a mesh axis runs over, the one named last changes fastest.
Arguments:
- residual: bfloat16 [4096, 4096], P('ctx', 'head'), may hold values from -84 to 84
- hyena_gain: float32 [4096], replicated, may hold values from 0.1 to 1.9
- in_weight: bfloat16 [4096, 3, 4096], P(None, None, 'head'), may hold values from -0.09375 to 0.09375
- short_filter: float32 [3, 3, 4096], P(None, None, 'head'), may hold values from -1 to 1
- decay_rate: float32 [4096, 16], P('head'), may hold values from 4.8828125e-05 to 0.033
- residue: float32 [4096, 16], P('head'), may hold values from -3 to 3
- skip_gain: float32 [4096], P('head'), may hold values from -1 to 1
- attn_gain: float32 [4096], replicated, may hold values from 0.1 to 1.9
- qkv_weight: bfloat16 [4096, 3, 2048], P(None, None, 'head'), may hold values from -0.1328125 to 0.1328125
Outputs:
- mixed: bfloat16 [4096, 4096], P('ctx', 'head')
- attended: bfloat16 [4096, 2048], P('ctx', 'head')
The draws below stay inside these ranges and needn't reach their ends.
All inputs are finite; a program needn't handle non-finite values.
Results may differ from the reference program's by a relative error of at most 0.02.
The reference program's roundings to bfloat16 on the way count: a program that leaves them out, or rounds other values in their place, can miss the bound.
Values may be sent and summed in bfloat16 or wider, within the bound.
A program may use at most 128 MiB of HBM per device.

```python
import math
import jax
import jax.numpy as jnp
from jax import lax

D = 4096
HD = 128
HEADS = 16
N_MODES = 16
TOKENS = 4096


def draw_residual(key, part):
    key = jax.random.fold_in(key, 11)
    base_key, row_key, col_key = jax.random.split(key, 3)
    ramp = jnp.exp(math.log(3.0) * (jnp.arange(D).astype(jnp.float32) / D - 0.5))
    base = jax.random.truncated_normal(base_key, -4.0, 4.0, (TOKENS, D), jnp.float32)
    rows = jnp.exp(jax.random.uniform(row_key, (TOKENS, 1), jnp.float32, math.log(0.3), math.log(3.0)))
    cols = jnp.exp(jax.random.uniform(col_key, (1, D), jnp.float32, math.log(0.4), math.log(4.0))) * ramp
    return (base * rows * cols).astype(jnp.bfloat16)


def draw_decay_rate(key, part):
    key = jax.random.fold_in(key, 12)
    slow_key = jax.random.fold_in(key, 1)
    low = math.log(0.2 / TOKENS)
    return jnp.exp(jax.random.uniform(slow_key, (D, N_MODES), jnp.float32, low, math.log(0.033)))


def draw_qkv_weight(key, part):
    key = jax.random.fold_in(key, 13)
    shape = (D, 3, HEADS * HD)
    base = jax.random.truncated_normal(key, -4.0, 4.0, shape, jnp.float32)
    return (base / math.sqrt(D)).astype(jnp.bfloat16)


def block_levels(rng, extent, cuts, low, high):
    level, own = 1.0, jax.random.fold_in(rng, 6)
    for axis_at, parts in cuts:
        heights = jnp.exp(jax.random.uniform(jax.random.fold_in(own, axis_at), (parts,), jnp.float32, low / len(cuts), high / len(cuts)))
        level = level * jnp.repeat(heights, extent[axis_at] // parts).reshape([-1 if axis == axis_at else 1 for axis in range(len(extent))])
    return level


def scatter_about(rng, extent, width, limit, cuts=(), dtype=jnp.bfloat16):
    level = block_levels(rng, extent, cuts, -0.22, 0.18) if cuts else 1.0
    values = jax.random.normal(rng, extent, jnp.float32) * width * level
    return jnp.minimum(jnp.maximum(values, -limit), limit).astype(dtype)


def setup_inputs(seed: int = 0) -> dict:
    seeds = jax.random.split(jax.random.key(seed), 10)
    residual = draw_residual(jax.random.fold_in(seeds[9], 71), 0)
    hyena_gain = jnp.clip(1.0 + 0.18 * jax.random.normal(seeds[1], (D,), jnp.float32), 0.1, 1.9)
    in_weight = scatter_about(seeds[2], (D, 3, D), D ** -0.5, 0.09375, ((2, 16),))
    short_filter = jnp.clip(jax.random.uniform(seeds[3], (3, 3, D), jnp.float32, -1.0, 1.0) * block_levels(seeds[3], (3, 3, D), ((2, 16),), -0.4, 0.0), -1.0, 1.0)
    decay_rate = draw_decay_rate(jax.random.fold_in(seeds[9], 71), 0)
    residue = scatter_about(seeds[5], (D, N_MODES), 0.5, 3.0, ((0, 16),), jnp.float32)
    skip_gain = jnp.clip(jax.random.uniform(seeds[6], (D,), jnp.float32, -1.0, 1.0) * block_levels(seeds[6], (D,), ((0, 16),), -0.4, 0.0), -1.0, 1.0)
    attn_gain = jnp.clip(1.0 + 0.18 * jax.random.normal(seeds[7], (D,), jnp.float32), 0.1, 1.9)
    qkv_weight = draw_qkv_weight(jax.random.fold_in(seeds[9], 71), 0)
    return {"residual": residual, "hyena_gain": hyena_gain, "in_weight": in_weight, "short_filter": short_filter, "decay_rate": decay_rate, "residue": residue, "skip_gain": skip_gain, "attn_gain": attn_gain, "qkv_weight": qkv_weight}


eps = 1e-06
rotary_base = 10000.0
highest = lax.Precision.HIGHEST

def combine_states(first_pair, second_pair):
    return (first_pair[0] * second_pair[0], second_pair[0] * first_pair[1] + second_pair[1])

def block_parts(product, decays, modal):
    span_len = 128 if product.shape[0] % 128 == 0 else product.shape[0]
    lag_steps = jnp.arange(span_len).astype(jnp.float32)
    filt_lags = jnp.einsum('cn,cnd->cd', modal, jnp.exp(-decays[:, :, None] * lag_steps), precision=highest)
    offsets = jnp.arange(span_len)[:, None] - jnp.arange(span_len)[None, :]
    toeplitz = jnp.where(offsets[None] >= 0, filt_lags[:, jnp.maximum(offsets, 0)], 0.0)
    block_count = product.shape[0] // span_len
    pieces = product.reshape(block_count, span_len, product.shape[1])
    intra = jnp.einsum('cts,bsc->btc', toeplitz, pieces, precision=highest).reshape(product.shape)
    tail_pows = jnp.exp(-decays[:, :, None] * (span_len - 1.0 - lag_steps))
    ends = jnp.einsum('bsc,cns->bcn', pieces, tail_pows, precision=highest)
    return (intra, ends, span_len)

def chain(ends, decays, span_len, state_zero):
    block_count = ends.shape[0]
    step_decay = jnp.broadcast_to(jnp.exp(-decays * span_len), ends.shape)
    inclusive = lax.associative_scan(combine_states, (step_decay, ends))[1]
    order = jnp.arange(block_count).astype(jnp.float32)
    powers = jnp.exp(-decays[None] * (span_len * order)[:, None, None])
    starts = jnp.concatenate([jnp.zeros_like(ends[:1]), inclusive[:-1]], axis=0) + powers * state_zero[None]
    final_state = inclusive[-1] + jnp.exp(-decays * (span_len * block_count)) * state_zero
    return (starts, final_state)

def spread(starts, decays, modal, span_len):
    lag_steps = jnp.arange(span_len).astype(jnp.float32)
    rise_table = modal[:, :, None] * jnp.exp(-decays[:, :, None] * (lag_steps + 1.0))
    return jnp.einsum('bcn,cnt->btc', starts, rise_table, precision=highest).reshape(-1, starts.shape[1])

def long_conv(product, decays, modal):
    intra, ends, span_len = block_parts(product, decays, modal)
    starts = chain(ends, decays, span_len, jnp.zeros(decays.shape, jnp.float32))[0]
    return intra + spread(starts, decays, modal, span_len)

def filter_coef(decay_rate, residue):
    return residue * jnp.sqrt(-jnp.expm1(-2.0 * decay_rate))

def short_conv(padded, taps):
    return taps[0] * padded[2:] + taps[1] * padded[1:-1] + taps[2] * padded[:-2]

def hyena_mix(streams, decays, modal, skip):
    product = streams[:, 1] * streams[:, 2]
    return streams[:, 0] * (long_conv(product, decays, modal) + skip * product)

def rotate(values, positions):
    half_dim = values.shape[-1] // 2
    inverse = jnp.exp(-jnp.log(rotary_base) * jnp.arange(half_dim).astype(jnp.float32) / half_dim)
    angle = positions[:, None] * inverse[None, :]
    cosine = jnp.cos(angle)[:, None, :]
    sine = jnp.sin(angle)[:, None, :]
    first_half = values[..., :half_dim]
    second_half = values[..., half_dim:]
    return jnp.concatenate([first_half * cosine - second_half * sine, second_half * cosine + first_half * sine], axis=-1)

def project(rows, gain, weight):
    rows_f = rows.astype(jnp.float32)
    scale_rows = lax.rsqrt(lax.optimization_barrier(jnp.mean(rows_f * rows_f, axis=1)) + eps)
    scaled = (rows_f * gain).astype(jnp.bfloat16)
    flat_weight = weight.reshape(weight.shape[0], -1)
    result = jnp.dot(scaled, flat_weight, preferred_element_type=jnp.float32) * scale_rows[:, None]
    return result.reshape(rows.shape[0], 3, -1)

def attend(queries, keys, values):
    length = queries.shape[0]
    span_len = min(1024, length)
    block_count = length // span_len
    factor = 1.0 / queries.shape[-1] ** 0.5

    def one_head(operands):
        head_q, head_k, head_v = operands

        def one_block(number):
            begin = (number * span_len).astype(jnp.int32)
            query_block = lax.dynamic_slice_in_dim(head_q, begin, span_len, 0)
            scores = jnp.dot(query_block, head_k.T, preferred_element_type=jnp.float32) * factor
            query_pos = begin + jnp.arange(span_len).astype(jnp.int32)
            key_pos = jnp.arange(length).astype(jnp.int32)
            scores = jnp.where(key_pos[None, :] <= query_pos[:, None], scores, -1e+30)
            weights = jnp.exp(scores - lax.optimization_barrier(jnp.max(scores, axis=1, keepdims=True)))
            totals = lax.optimization_barrier(jnp.sum(weights, axis=1, keepdims=True))
            return jnp.dot(weights.astype(jnp.bfloat16), head_v, preferred_element_type=jnp.float32) / totals
        return lax.map(one_block, jnp.arange(block_count).astype(jnp.int32)).reshape(length, -1)
    outputs = lax.map(one_head, (queries.transpose(1, 0, 2), keys.transpose(1, 0, 2), values.transpose(1, 0, 2)))
    return outputs.transpose(1, 0, 2).reshape(length, -1).astype(jnp.bfloat16)

def reference(residual, hyena_gain, in_weight, short_filter, decay_rate, residue, skip_gain, attn_gain, qkv_weight):
    streams = project(residual, hyena_gain, in_weight).astype(jnp.bfloat16)
    padded = jnp.pad(streams.astype(jnp.float32), ((2, 0), (0, 0), (0, 0)))
    modal = filter_coef(decay_rate, residue)
    gated = hyena_mix(short_conv(padded, short_filter), decay_rate, modal, skip_gain)
    mixed = (residual.astype(jnp.float32) + gated).astype(jnp.bfloat16)
    projected = project(mixed, attn_gain, qkv_weight).reshape(TOKENS, 3, HEADS, HD)
    positions = jnp.arange(TOKENS).astype(jnp.float32)
    queries = rotate(projected[:, 0], positions).astype(jnp.bfloat16)
    keys = rotate(projected[:, 1], positions).astype(jnp.bfloat16)
    values = projected[:, 2].astype(jnp.bfloat16)
    attended = attend(queries, keys, values)
    return (mixed, attended)
```

```python
import functools

import jax
import jax.numpy as jnp
import numpy as np
from jax import lax
from jax.experimental import pallas as pl
from jax.experimental.pallas import tpu as pltpu
from jax.sharding import PartitionSpec as P

MESH = pl.DeviceIdType.MESH
f32 = jnp.float32
bf16 = jnp.bfloat16

HD = 128
EPS = 1e-6
ROWS = 256
WIDTH = 256
NH = 16
NC = 16
NZ = 8
MODES = 16
SPAN = 32
CHUNKS = 8
XFIRST = 112


def rope_tables():
    half = HD // 2
    inverse = 10000.0 ** (-np.arange(half) / half)

    def table(positions):
        angle = positions[:, None] * inverse[None, :]
        cos, sin = np.cos(angle), np.sin(angle)
        return np.concatenate([cos, cos, sin, sin], axis=1).astype(np.float32)

    return table(np.arange(NC) * float(ROWS)), table(np.arange(ROWS) * 1.0)


def kernel(
    res, hgain, w1, taps, decay, residue, skip, again, w2, far, near,
    mixed, attended,
    g1, g2, w1s, w2s, acc1, acc2, sq, strm, halo_out, halo_in,
    mode_a, mode_p, mode_f, modal, upad, qs, conv, ends, gate, e_out, e_in,
    cs, qrot, kv, kvs, m_s, l_s, o_s,
    wsem, gs, gr, hsem, es, er, ks, kr, fs,
):
    c = lax.axis_index("ctx")
    h = lax.axis_index("head")
    core = lax.rem(c, 2)
    sgn = 1 - 2 * core
    z = lax.rem(h, NZ)
    xh = h // NZ
    chip = c // 2

    def head(x, zz):
        return x * NZ + lax.rem(zz + 2 * NZ, NZ)

    partner = head(1 - xh, z)
    ahead = head(xh, z + sgn)
    behind = head(xh, z - sgn)

    wcopies = []
    for j in range(3):
        wcopies.append(pltpu.make_async_copy(w1.at[j], w1s.at[:, pl.ds(j * WIDTH, WIDTH)], wsem.at[j]))
    for j in range(3):
        wcopies.append(pltpu.make_async_copy(w2.at[j], w2s.at[:, pl.ds(j * HD, HD)], wsem.at[3 + j]))
    for copy in wcopies:
        copy.start()

    barrier = pltpu.get_barrier_semaphore()
    for to in (partner, ahead, behind):
        pl.semaphore_signal(barrier, inc=1, device_id={"head": to}, device_id_type=MESH)
    for k in range(1, NC):
        pl.semaphore_signal(
            barrier, inc=1, device_id={"ctx": lax.rem(c + k, NC)}, device_id_type=MESH
        )
    pl.semaphore_wait(barrier, NC + 2)

    sends = []
    parts = ((ROWS - XFIRST, XFIRST), (0, ROWS - XFIRST))

    def gather(own, g, which, prepare, fold):
        count = [0]

        def copy(part, org, to, index, src=None):
            lo, n = parts[part]
            dst = g.at[org, pl.ds(lo, n)]
            return pltpu.make_async_remote_copy(
                src_ref=dst if src is None else src.at[pl.ds(lo, n)],
                dst_ref=dst,
                send_sem=gs.at[which, index],
                recv_sem=gr.at[which, part, org],
                device_id={"head": to},
                device_id_type=MESH,
            )

        def send(part, org, to, src=None):
            one = copy(part, org, to, count[0], src)
            count[0] += 1
            one.start()
            sends.append(one)

        def wait(part, org):
            copy(part, org, partner, 0).wait_recv()

        send(0, h, partner, own)
        send(0, h, ahead, own)
        send(0, h, behind, own)
        send(1, h, ahead, own)
        send(1, h, behind, own)
        send(1, h, partner, own)
        prepare()
        fold(h, own, True)
        wait(0, partner)
        send(0, partner, behind)
        send(0, partner, ahead)
        late = [partner]
        for d in range(1, 5):
            a, b = head(xh, z - sgn * d), head(xh, z + sgn * d)
            a2, b2 = head(1 - xh, z - sgn * d), head(1 - xh, z + sgn * d)
            wait(0, a)
            if d < 4:
                send(0, a, ahead)
                wait(0, b)
            if d < 3:
                send(0, b, behind)
            wait(1, a)
            if d < 4:
                send(1, a, ahead)
            send(1, a, partner)
            if d < 4:
                wait(1, b)
                if d < 3:
                    send(1, b, behind)
                send(1, b, partner)
            wait(0, b2)
            if d < 4:
                send(0, b2, behind)
                wait(0, a2)
            if d < 3:
                send(0, a2, ahead)
            fold(a, g.at[a], False)
            if d < 4:
                fold(b, g.at[b], False)
            for org in late:
                wait(1, org)
                fold(org, g.at[org], False)
            late = [b2] if d == 4 else [a2, b2]
        for org in late:
            wait(1, org)
            fold(org, g.at[org], False)

    def folder(gain, w, acc):
        def fold(org, ref, first):
            columns = pl.ds(pl.multiple_of(org * WIDTH, WIDTH), WIDTH)
            rows = ref[...].astype(f32)
            squares = rows * rows
            squares = squares[:, :128] + squares[:, 128:]
            scaled = (rows * gain[:, columns]).astype(bf16)
            product = jnp.dot(scaled, w[columns, :], preferred_element_type=f32)
            if first:
                sq[...] = squares
                acc[...] = product
            else:
                sq[...] += squares
                acc[...] += product

        return fold

    def row_scale(lo, n):
        total = jnp.sum(sq[pl.ds(lo, n), :], axis=1, keepdims=True)
        return lax.rsqrt(total * (1.0 / (NH * WIDTH)) + EPS)

    def tables():
        d = decay[...]
        a = jnp.exp(-d)
        mode_a[...] = a
        twice = 2.0 * d
        series = twice * (1.0 - twice * (0.5 - twice * (1.0 / 6 - twice * (1.0 / 24 - twice * (1.0 / 120)))))
        coef = residue[...] * jnp.sqrt(jnp.where(twice < 0.1, series, 1.0 - jnp.exp(-twice)))
        modal[...] = coef
        steps = lax.broadcasted_iota(jnp.int32, (CHUNKS, WIDTH), 0).astype(f32)
        for n in range(MODES):
            mode_p[n] = jnp.exp(-decay[pl.ds(n, 1), :] * (steps * SPAN))
        lags = lax.broadcasted_iota(jnp.int32, (SPAN, WIDTH), 0).astype(f32)
        filt = jnp.zeros((SPAN, WIDTH), f32)
        for n in range(MODES):
            filt = filt + modal[pl.ds(n, 1), :] * jnp.exp(-decay[pl.ds(n, 1), :] * lags)
        filt = filt + jnp.where(lags == 0.0, skip[...], 0.0)
        for t in range(SPAN):
            mode_f[t] = jnp.broadcast_to(filt[t : t + 1, :], (CHUNKS, WIDTH))
        upad[pl.ds(0, SPAN)] = jnp.zeros((SPAN, CHUNKS, WIDTH), f32)
        there = far[c]
        fc, fsn = there[:, :HD], there[:, HD:]
        nc, ns = near[:, pl.ds(0, HD)], near[:, pl.ds(HD, HD)]
        cs[:, pl.ds(0, HD)] = nc * fc - ns * fsn
        lane = lax.broadcasted_iota(jnp.int32, (ROWS, HD), 1)
        sine = ns * fc + nc * fsn
        cs[:, pl.ds(HD, HD)] = jnp.where(lane < HD // 2, -sine, sine)

    def before_first():
        tables()
        for copy in wcopies[:3]:
            copy.wait()

    gather(res, g1, 0, before_first, folder(hgain, w1s, acc1))

    for k in range(6):
        strm[k, pl.ds(0, 8), :] = jnp.zeros((8, 128), f32)
    last = ROWS - 16
    halo_out[...] = (acc1[pl.ds(last, 16), :] * row_scale(last, 16)).astype(bf16)
    halo = pltpu.make_async_remote_copy(
        src_ref=halo_out, dst_ref=halo_in, send_sem=hsem.at[0], recv_sem=hsem.at[1],
        device_id={"ctx": lax.rem(c + 1, NC)}, device_id_type=MESH,
    )
    halo.start()

    def to_streams(i, _):
        lo = pl.multiple_of(i * 32, 32)
        block = (acc1[pl.ds(lo, 32), :] * row_scale(lo, 32)).astype(bf16)
        block = block.astype(f32)
        for k in range(6):
            strm[k, pl.ds(lo + 8, 32), :] = block[:, k * 128 : (k + 1) * 128]
        return 0

    lax.fori_loop(0, ROWS // 32, to_streams, 0)

    def tap(j, s):
        return taps[j, pl.ds(s, 1), :]

    def stream_rows(start):
        return jnp.concatenate(
            [strm[k, pl.ds(start, CHUNKS, stride=SPAN), :] for k in range(6)], axis=1
        )

    def short(now, one, two):
        out = []
        for s in range(3):
            cols = slice(s * WIDTH, (s + 1) * WIDTH)
            out.append(tap(0, s) * now[:, cols] + tap(1, s) * one[:, cols] + tap(2, s) * two[:, cols])
        return out

    def short_step(s, _):
        q, k, v = short(stream_rows(s + 8), stream_rows(s + 7), stream_rows(s + 6))
        qs[s] = q
        upad[SPAN + s] = k * v
        return 0

    lax.fori_loop(2, SPAN, short_step, 0)
    halo.wait_recv()
    before = jnp.where(c == 0, 0.0, halo_in[...].astype(f32)[8:16, :])
    for k in range(6):
        strm[k, pl.ds(0, 8), :] = before[:, k * 128 : (k + 1) * 128]
    lax.fori_loop(0, 2, short_step, 0)

    def horner(s, state):
        u = upad[SPAN + s]
        return tuple(state[n] * mode_a[pl.ds(n, 1), :] + u for n in range(MODES))

    zero = jnp.zeros((CHUNKS, WIDTH), f32)
    state = lax.fori_loop(0, SPAN, horner, (zero,) * MODES)
    sub = lax.broadcasted_iota(jnp.int32, (CHUNKS, WIDTH), 0)
    for n in range(MODES):
        e = state[n]
        for k in (1, 2, 4):
            moved = jnp.where(sub >= k, pltpu.roll(e, k, 0), 0.0)
            e = e + mode_p[n, pl.ds(k, 1), :] * moved
        e_out[pl.ds(n, 1), :] = e[CHUNKS - 1 : CHUNKS, :]
        ends[n] = jnp.where(sub >= 1, pltpu.roll(e, 1, 0), 0.0)

    def state_copy(j):
        return pltpu.make_async_remote_copy(
            src_ref=e_out, dst_ref=e_in.at[c], send_sem=es.at[j], recv_sem=er.at[c],
            device_id={"ctx": j}, device_id_type=MESH,
        )

    for j in range(1, NC):

        @pl.when(j > c)
        def _():
            state_copy(j).start()

    for block in range(SPAN // 8):

        def lag(d, total):
            return total + mode_f[d][None] * upad[pl.ds(SPAN + block * 8 - d, 8)]

        conv[pl.ds(block * 8, 8)] = lax.fori_loop(
            0, block * 8 + 8, lag, jnp.zeros((8, CHUNKS, WIDTH), f32)
        )

    whole = jnp.exp(-decay[...] * float(ROWS))

    def arrive(i, total):
        pltpu.make_async_remote_copy(
            src_ref=e_out, dst_ref=e_in.at[i], send_sem=es.at[0], recv_sem=er.at[i],
            device_id={"ctx": 0}, device_id_type=MESH,
        ).wait_recv()
        return total * whole + e_in[i]

    inward = lax.fori_loop(0, c, arrive, jnp.zeros((MODES, WIDTH), f32))
    rise = modal[...] * mode_a[...]
    begin = tuple(
        (ends[n] + inward[n : n + 1, :] * mode_p[n]) * rise[n : n + 1, :] for n in range(MODES)
    )

    def spread(t, state):
        total = conv[t]
        for n in range(MODES):
            total = total + state[n]
        gated = qs[t] * total
        for k in range(2):
            gate[k, pl.ds(t, CHUNKS, stride=SPAN), :] = gated[:, k * 128 : (k + 1) * 128]
        return tuple(state[n] * mode_a[pl.ds(n, 1), :] for n in range(MODES))

    lax.fori_loop(0, SPAN, spread, begin)
    for k in range(2):
        cols = pl.ds(k * 128, 128)
        mixed[:, cols] = (res[:, cols].astype(f32) + gate[k]).astype(bf16)

    def before_second():
        for copy in wcopies[3:]:
            copy.wait()

    gather(mixed, g2, 1, before_second, folder(again, w2s, acc2))

    def finish(i, _):
        lo = pl.multiple_of(i * 32, 32)
        rows = acc2[pl.ds(lo, 32), :] * row_scale(lo, 32)
        cosine, sine = cs[pl.ds(lo, 32), pl.ds(0, HD)], cs[pl.ds(lo, 32), pl.ds(HD, HD)]

        def turn(x):
            return (x * cosine + pltpu.roll(x, HD // 2, 1) * sine).astype(bf16)

        qrot[pl.ds(lo, 32), :] = turn(rows[:, :HD])
        kv[pl.ds(lo, 32), pl.ds(0, HD)] = turn(rows[:, HD : 2 * HD])
        kv[pl.ds(lo, 32), pl.ds(HD, HD)] = rows[:, 2 * HD :].astype(bf16)
        return 0

    lax.fori_loop(0, ROWS // 32, finish, 0)

    def kv_copy(src, org, sem, to):
        return pltpu.make_async_remote_copy(
            src_ref=src, dst_ref=kvs.at[org], send_sem=sem, recv_sem=kr.at[org],
            device_id={"ctx": to}, device_id_type=MESH,
        )

    sibling = c + sgn

    @pl.when(core == 0)
    def _():
        kv_copy(kv, c, ks.at[0], sibling).start()

    for j in range(1, NC // 2):

        @pl.when(j > chip)
        def _():
            kv_copy(kv, c, ks.at[j], 2 * j + core).start()

    factor = 1.0 / HD**0.5

    def attend(ref, diagonal, first):
        scores = (
            lax.dot_general(
                qrot[...], ref[:, pl.ds(0, HD)], (((1,), (1,)), ((), ())), preferred_element_type=f32
            )
            * factor
        )
        if diagonal:
            row = lax.broadcasted_iota(jnp.int32, scores.shape, 0)
            col = lax.broadcasted_iota(jnp.int32, scores.shape, 1)
            scores = jnp.where(col <= row, scores, -1e30)
        best = jnp.max(scores, axis=1, keepdims=True)
        if not first:
            best = jnp.maximum(best, m_s[:, pl.ds(0, 1)])
        weights = jnp.exp(scores - best)
        sums = jnp.sum(weights, axis=1, keepdims=True)
        update = jnp.dot(weights.astype(bf16), ref[:, pl.ds(HD, HD)], preferred_element_type=f32)
        if first:
            l_s[...] = jnp.broadcast_to(sums, l_s.shape)
            o_s[...] = update
        else:
            rescale = jnp.exp(m_s[...] - best)
            l_s[...] = l_s[...] * rescale + sums
            o_s[...] = o_s[...] * rescale + update
        m_s[...] = jnp.broadcast_to(best, m_s.shape)

    attend(kv, True, True)

    @pl.when(core == 1)
    def _():
        kv_copy(kv, c - 1, ks.at[0], 0).wait_recv()
        attend(kvs.at[c - 1], False, False)

    def earlier(k, _):
        org = 2 * (chip - 1 - k) + core
        other = org + sgn
        kv_copy(kv, org, ks.at[0], sibling).wait_recv()
        kv_copy(kvs.at[org], org, fs.at[k], sibling).start()
        attend(kvs.at[org], False, False)
        kv_copy(kv, other, ks.at[0], sibling).wait_recv()
        attend(kvs.at[other], False, False)
        return 0

    lax.fori_loop(0, chip, earlier, 0)
    attended[...] = (o_s[...] / l_s[...]).astype(bf16)

    for one in sends:
        one.wait_send()
    halo.wait_send()
    for j in range(1, NC):

        @pl.when(j > c)
        def _():
            state_copy(j).wait_send()

    @pl.when(core == 0)
    def _():
        kv_copy(kv, c, ks.at[0], sibling).wait_send()

    for j in range(1, NC // 2):

        @pl.when(j > chip)
        def _():
            kv_copy(kv, c, ks.at[j], 2 * j + core).wait_send()

    def passed(k, _):
        org = 2 * (chip - 1 - k) + core
        kv_copy(kvs.at[org], org, fs.at[k], sibling).wait_send()
        return 0

    lax.fori_loop(0, chip, passed, 0)


def local(residual, hyena_gain, in_weight, short_filter, decay_rate, residue, skip_gain, attn_gain, qkv_weight):
    far, near = rope_tables()
    vmem = pl.BlockSpec(memory_space=pltpu.VMEM)
    hbm = pl.BlockSpec(memory_space=pl.ANY)
    dma = pltpu.SemaphoreType.DMA
    return pl.pallas_call(
        kernel,
        out_shape=(
            jax.ShapeDtypeStruct((ROWS, WIDTH), bf16),
            jax.ShapeDtypeStruct((ROWS, HD), bf16),
        ),
        in_specs=[vmem, vmem, hbm, vmem, vmem, vmem, vmem, vmem, hbm, vmem, vmem],
        out_specs=(vmem, vmem),
        scratch_shapes=[
            pltpu.VMEM((NH, ROWS, WIDTH), bf16),
            pltpu.VMEM((NH, ROWS, WIDTH), bf16),
            pltpu.VMEM((NH * WIDTH, 3 * WIDTH), bf16),
            pltpu.VMEM((NH * WIDTH, 3 * HD), bf16),
            pltpu.VMEM((ROWS, 3 * WIDTH), f32),
            pltpu.VMEM((ROWS, 3 * HD), f32),
            pltpu.VMEM((ROWS, 128), f32),
            pltpu.VMEM((6, ROWS + 8, 128), f32),
            pltpu.VMEM((16, 3 * WIDTH), bf16),
            pltpu.VMEM((16, 3 * WIDTH), bf16),
            pltpu.VMEM((MODES, WIDTH), f32),
            pltpu.VMEM((MODES, CHUNKS, WIDTH), f32),
            pltpu.VMEM((SPAN, CHUNKS, WIDTH), f32),
            pltpu.VMEM((MODES, WIDTH), f32),
            pltpu.VMEM((2 * SPAN, CHUNKS, WIDTH), f32),
            pltpu.VMEM((SPAN, CHUNKS, WIDTH), f32),
            pltpu.VMEM((SPAN, CHUNKS, WIDTH), f32),
            pltpu.VMEM((MODES, CHUNKS, WIDTH), f32),
            pltpu.VMEM((2, ROWS, 128), f32),
            pltpu.VMEM((MODES, WIDTH), f32),
            pltpu.VMEM((NC, MODES, WIDTH), f32),
            pltpu.VMEM((ROWS, 2 * HD), f32),
            pltpu.VMEM((ROWS, HD), bf16),
            pltpu.VMEM((ROWS, 2 * HD), bf16),
            pltpu.VMEM((NC, ROWS, 2 * HD), bf16),
            pltpu.VMEM((ROWS, HD), f32),
            pltpu.VMEM((ROWS, HD), f32),
            pltpu.VMEM((ROWS, HD), f32),
            dma((6,)),
            dma((2, 32)),
            dma((2, 2, NH)),
            dma((2,)),
            dma((NC,)),
            dma((NC,)),
            dma((NC // 2,)),
            dma((NC,)),
            dma((NC // 2,)),
        ],
        compiler_params=pltpu.CompilerParams(
            collective_id=1, has_side_effects=True, vmem_limit_bytes=48 << 20
        ),
        name="genome",
    )(
        residual,
        hyena_gain.reshape(1, -1),
        in_weight.transpose(1, 0, 2),
        short_filter,
        decay_rate.T,
        residue.T,
        skip_gain.reshape(1, -1),
        attn_gain.reshape(1, -1),
        qkv_weight.transpose(1, 0, 2),
        far.reshape(NC, 1, -1),
        near,
    )


def solution(mesh):
    return jax.shard_map(
        local,
        mesh=mesh,
        in_specs=(
            P("ctx", "head"),
            P(),
            P(None, None, "head"),
            P(None, None, "head"),
            P("head", None),
            P("head", None),
            P("head"),
            P(),
            P(None, None, "head"),
        ),
        out_specs=(P("ctx", "head"), P("ctx", "head")),
        check_vma=False,
    )
```

```python
import functools

import jax
import jax.numpy as jnp
import numpy as np
from jax import lax
from jax.experimental import pallas as pl
from jax.experimental.pallas import tpu as pltpu
from jax.sharding import PartitionSpec as P

MESH = pl.DeviceIdType.MESH
f32 = jnp.float32
bf16 = jnp.bfloat16

HD = 128
EPS = 1e-6
ROWS = 256
WIDTH = 256
NH = 16
NC = 16
NZ = 8
MODES = 16
SPAN = 32
CHUNKS = 8
STOP = 9
NOATT = 0
TREE = (0, 1)
DESC = 1
UN = 4
LAG0 = 8
LAG1 = 3
NOFOLD = 0
DIST = 4
PARTS1 = (((0, 80, 0), (80, 48, 1), (128, 80, 0), (208, 48, 1)),)
PARTS2 = (((0, 80, 0), (80, 48, 1)), ((128, 80, 0), (208, 48, 1)))
GROUP = 128
KVORDER = 1


def rope_tables():
    half = HD // 2
    inverse = 10000.0 ** (-np.arange(half) / half)

    def table(positions):
        angle = positions[:, None] * inverse[None, :]
        cos, sin = np.cos(angle), np.sin(angle)
        return np.concatenate([cos, cos, sin, sin], axis=1).astype(np.float32)

    return table(np.arange(NC) * float(ROWS)), table(np.arange(ROWS) * 1.0)


def kernel(
    res_h, hgain_h, w1, taps_h, decay_h, residue_h, skip_h, again_h, w2, far_h, near_h,
    mixed, attended,
    hgain, taps, decay, residue, skip, again, far, near,
    g1, g2, w1s, w2s, acc1, acc2, sq, strm, halo_out, halo_in,
    mode_a, mode_b, mode_p, mode_f, modal, upad, qs, conv, ends, gate, e_out, e_in, s_out, s_in,
    cs, qt, kv, kvs, m_s, l_s, o_s, att,
    psem, osem, asem, wsem, gs, gr, hsem, ssem, es, er, ks, kr, fs, rs,
):
    c = lax.axis_index("ctx")
    h = lax.axis_index("head")
    core = lax.rem(c, 2)
    sgn = 1 - 2 * core
    z = lax.rem(h, NZ)
    xh = h // NZ
    chip = c // 2

    def head(x, zz):
        return x * NZ + lax.rem(zz + 2 * NZ, NZ)

    partner = head(1 - xh, z)
    ahead = head(xh, z + sgn)
    behind = head(xh, z - sgn)

    small = ((res_h, g1.at[h]), (decay_h, decay), (residue_h, residue), (skip_h, skip), (hgain_h, hgain),
             (taps_h, taps), (far_h, far), (near_h, near), (again_h, again))
    scopies = [pltpu.make_async_copy(a, b, psem.at[k]) for k, (a, b) in enumerate(small)]
    for copy in scopies:
        copy.start()
    wcopies = []
    for j in range(3):
        wcopies.append(pltpu.make_async_copy(w1.at[j], w1s.at[:, pl.ds(j * WIDTH, WIDTH)], wsem.at[j]))
    for j in range(3):
        wcopies.append(pltpu.make_async_copy(w2.at[j], w2s.at[:, pl.ds(j * HD, HD)], wsem.at[3 + j]))
    for copy in wcopies:
        copy.start()

    barrier = pltpu.get_barrier_semaphore()
    slant, slant_back = head(1 - xh, z + sgn), head(1 - xh, z - sgn)
    for to in (partner, ahead, behind, slant, slant_back):
        pl.semaphore_signal(barrier, inc=1, device_id={"head": to}, device_id_type=MESH)
    for k in range(1, NC // 2):
        to = 2 * lax.rem(chip + k, NC // 2) + core
        pl.semaphore_signal(barrier, inc=1, device_id={"ctx": to}, device_id_type=MESH)
    for k in (1, NC - 1):
        pl.semaphore_signal(
            barrier, inc=1, device_id={"ctx": lax.rem(c + k, NC)}, device_id_type=MESH
        )
    pl.semaphore_wait(barrier, 5 + NC // 2 - 1 + 2)
    scopies[0].wait()


    def gather(g, which, groups, prepare, fold, done):
        numbers, count = [], 0
        for group in groups:
            numbers.append(range(count, count + len(group)))
            count += len(group)
        flat = [part for group in groups for part in group]

        def copy(p, org, to):
            rows = g.at[org, pl.ds(flat[p][0], flat[p][1])]
            return pltpu.make_async_remote_copy(
                src_ref=rows, dst_ref=rows, send_sem=gs.at[which, p], recv_sem=gr.at[which, p, org],
                device_id={"head": to}, device_id_type=MESH,
            )

        def send(p, org, to):
            copy(p, org, to).start()

        def wait(p, org):
            copy(p, org, partner).wait_recv()

        def begin(n):
            for p in numbers[n]:
                if flat[p][2]:
                    send(p, h, slant)
                    send(p, h, slant_back)
            for p in numbers[n]:
                send(p, h, ahead)
                send(p, h, behind)
            for p in numbers[n]:
                send(p, h, partner)

        def step(n, d, between=lambda j: None):
            a, b = head(xh, z - sgn * d), head(xh, z + sgn * d)
            a2, b2 = head(1 - xh, z - sgn * d), head(1 - xh, z + sgn * d)

            def hop(p, org, to, far, over):
                wait(p, org)

                @pl.when(d < far)
                def _():
                    send(p, org, to)
                    if over and far == 3:
                        send(p, org, partner)

                if over and far == 3:

                    @pl.when(d == 3)
                    def _():
                        send(p, org, partner)

                if over and far == 4:

                    @pl.when(d == 3)
                    def _():
                        send(p, org, slant)

                    @pl.when(d < 4)
                    def _():
                        send(p, org, partner)

            def both(p, first, second, to, back, over):
                hop(p, first, to, 4, over)

                @pl.when(d < 4)
                def _():
                    hop(p, second, back, 3, over)

            calls = [(p, a, b, ahead, behind, not flat[p][2]) for p in numbers[n]]
            calls += [(p, b2, a2, behind, ahead, False) for p in numbers[n] if flat[p][2]]
            for i, call in enumerate(calls):
                both(*call)
                for j in range(4 * i // len(calls), 4 * (i + 1) // len(calls)):
                    between(j)

        def folds(n, d):
            def one(j):
                over = j >= jnp.where(d == 1, 3, jnp.where(d == 4, 1, 2))
                here = jnp.where(d == 1, j, 2 * d - 1 + j)
                there = jnp.where(d == 1, 0, jnp.where(d == 4, 4 + j, 2 * d - 5 + j))
                k = jnp.where(over, there, here)
                apart = jnp.where(k % 2 == 1, -((k + 1) // 2), k // 2)
                org = head(jnp.where(over, 1 - xh, xh), z + sgn * apart)

                @pl.when(over)
                def _():
                    for p in numbers[n]:
                        if not flat[p][2]:
                            wait(p, org)

                @pl.when(jnp.logical_and(over, k == 0))
                def _():
                    for p in numbers[n]:
                        if flat[p][2]:
                            wait(p, org)

                if not NOFOLD:
                    fold(groups[n], org)

            return one

        def all_folds(n, d):
            one = folds(n, d)

            def body(j, _):
                one(j)
                return 0

            lax.fori_loop(0, 4, body, 0)

        lag = len(groups) > 1
        for n in range(len(groups)):
            begin(n)
        step(0, 1)
        prepare()

        def later(d, _):
            step(0, d, folds(0, d - 1))
            if lag:
                step(1, d - 1)

                @pl.when(d > 2)
                def _():
                    all_folds(1, d - 2)

            return 0

        lax.fori_loop(2, 5, later, 0)
        all_folds(0, 4)
        done(0)
        if lag:
            all_folds(1, 3)
            step(1, 4)
            all_folds(1, 4)
            done(1)

    def sent(g, which, groups):
        for p, part in enumerate(part for group in groups for part in group):
            rows = g.at[pl.ds(0, NH - 1), pl.ds(part[0], part[1])]
            pltpu.make_async_remote_copy(
                src_ref=rows, dst_ref=rows, send_sem=gs.at[which, p], recv_sem=gr.at[which, p, 0],
                device_id={"head": partner}, device_id_type=MESH,
            ).wait_send()

    def folder(g, gain, w, acc):
        def fold(group, org):
            lo, n = group[0][0], sum(part[1] for part in group)
            here = pl.ds(lo, n)
            columns = pl.ds(pl.multiple_of(org * WIDTH, WIDTH), WIDTH)
            rows = g[org, here].astype(f32)
            squares = rows * rows
            sq[here, :] += squares[:, :128] + squares[:, 128:]
            scaled = (rows * gain[:, columns]).astype(bf16)
            acc[here, :] += jnp.dot(scaled, w[columns, :], preferred_element_type=f32)

        return fold

    def row_scale(lo, n):
        total = jnp.sum(sq[pl.ds(lo, n), :], axis=1, keepdims=True)
        return lax.rsqrt(total * (1.0 / (NH * WIDTH)) + EPS)

    def tables():
        d = decay[...]
        a = jnp.exp(-d)
        mode_a[...] = a
        twice = 2.0 * d
        series = twice * (1.0 - twice * (0.5 - twice * (1.0 / 6 - twice * (1.0 / 24 - twice * (1.0 / 120)))))
        coef = residue[...] * jnp.sqrt(jnp.where(twice < 0.1, series, 1.0 - jnp.exp(-twice)))
        modal[...] = coef
        steps = lax.broadcasted_iota(jnp.int32, (CHUNKS, WIDTH), 0).astype(f32)
        for n in range(MODES):
            mode_b[n] = jnp.broadcast_to(mode_a[pl.ds(n, 1), :], (CHUNKS, WIDTH))
            mode_p[n] = jnp.exp(-decay[pl.ds(n, 1), :] * (steps * SPAN))
        lags = lax.broadcasted_iota(jnp.int32, (SPAN, WIDTH), 0).astype(f32)
        filt = jnp.zeros((SPAN, WIDTH), f32)
        for n in range(MODES):
            filt = filt + modal[pl.ds(n, 1), :] * jnp.exp(-decay[pl.ds(n, 1), :] * lags)
        filt = filt + jnp.where(lags == 0.0, skip[...], 0.0)
        for t in range(SPAN):
            mode_f[t] = jnp.broadcast_to(filt[t : t + 1, :], (CHUNKS, WIDTH))
        upad[pl.ds(0, SPAN)] = jnp.zeros((SPAN, CHUNKS, WIDTH), f32)
        there = far[c]
        fc, fsn = there[:, :HD], there[:, HD:]
        nc, ns = near[:, pl.ds(0, HD)], near[:, pl.ds(HD, HD)]
        cs[:, pl.ds(0, HD)] = nc * fc - ns * fsn
        lane = lax.broadcasted_iota(jnp.int32, (ROWS, HD), 1)
        sine = ns * fc + nc * fsn
        cs[:, pl.ds(HD, HD)] = jnp.where(lane < HD // 2, -sine, sine)

    def before_first():
        for copy in scopies[1:]:
            copy.wait()
        tables()
        sq[...] = jnp.zeros_like(sq)
        acc1[...] = jnp.zeros_like(acc1)
        for copy in wcopies[:3]:
            copy.wait()

    if STOP < 1:
        before_first()
    if STOP >= 1:
        gather(g1, 0, PARTS1, before_first, folder(g1, hgain, w1s, acc1), lambda n: None)

    if STOP >= 2:
        last = ROWS - 16
        halo_out[...] = (acc1[pl.ds(last, 16), :] * row_scale(last, 16)).astype(bf16)
        halo = pltpu.make_async_remote_copy(
            src_ref=halo_out, dst_ref=halo_in, send_sem=hsem.at[0], recv_sem=hsem.at[1],
            device_id={"ctx": lax.rem(c + 1, NC)}, device_id_type=MESH,
        )
        halo.start()
        for k in range(6):
            strm[k, pl.ds(0, 8), :] = jnp.zeros((8, 128), f32)

        def to_streams(i, _):
            lo = pl.multiple_of(i * 32, 32)
            block = (acc1[pl.ds(lo, 32), :] * row_scale(lo, 32)).astype(bf16)
            block = block.astype(f32)
            for k in range(6):
                strm[k, pl.ds(lo + 8, 32), :] = block[:, k * 128 : (k + 1) * 128]
            return 0

        lax.fori_loop(0, ROWS // 32, to_streams, 0)

        def tap(j, s):
            return taps[j, pl.ds(s, 1), :]

        def stream_rows(start):
            return jnp.concatenate(
                [strm[k, pl.ds(start, CHUNKS, stride=SPAN), :] for k in range(6)], axis=1
            )

        def short(now, one, two):
            out = []
            for s in range(3):
                cols = slice(s * WIDTH, (s + 1) * WIDTH)
                out.append(tap(0, s) * now[:, cols] + tap(1, s) * one[:, cols] + tap(2, s) * two[:, cols])
            return out

        def short_step(s, _):
            q, k, v = short(stream_rows(s + 8), stream_rows(s + 7), stream_rows(s + 6))
            qs[s] = q
            upad[SPAN + s] = k * v
            return 0

        lax.fori_loop(0, SPAN, short_step, 0, unroll=UN)

    if STOP >= 3:
        def horner(s, state):
            u = upad[SPAN + s]
            return tuple(state[n] * mode_b[n] + u for n in range(MODES))

        zero = jnp.zeros((CHUNKS, WIDTH), f32)
        state = lax.fori_loop(0, SPAN, horner, (zero,) * MODES, unroll=UN)
        sub = lax.broadcasted_iota(jnp.int32, (CHUNKS, WIDTH), 0)
        for n in range(MODES):
            e = state[n]
            for k in (1, 2, 4):
                moved = jnp.where(sub >= k, pltpu.roll(e, k, 0), 0.0)
                e = e + mode_p[n, pl.ds(k, 1), :] * moved
            e_out[pl.ds(n, 1), :] = e[CHUNKS - 1 : CHUNKS, :]
            ends[n] = jnp.where(sub >= 1, pltpu.roll(e, 1, 0), 0.0)

        def inside(block):
            def lag(d, total):
                return total + mode_f[d][None] * upad[pl.ds(SPAN + block * 8 - d, 8)]

            conv[pl.ds(block * 8, 8)] = lax.fori_loop(
                0, block * 8 + 8, lag, jnp.zeros((8, CHUNKS, WIDTH), f32), unroll=UN
            )

        for block in range(3):
            inside(block)

        halo.wait_recv()
        before = jnp.where(c == 0, 0.0, halo_in[...].astype(f32)[14:16, :])
        first, second = [], []
        for s in range(3):
            two, one = (before[r : r + 1, s * WIDTH : (s + 1) * WIDTH] for r in range(2))
            now, then = (
                jnp.concatenate([strm[2 * s + k, pl.ds(8 + r, 1), :] for k in range(2)], axis=1)
                for r in range(2)
            )
            base = tap(0, s) * now
            first.append((base, tap(1, s) * one + tap(2, s) * two))
            base = tap(0, s) * then + tap(1, s) * now
            second.append((base, tap(2, s) * one))

        def product(pair):
            (k, dk), (v, dv) = pair[1:]
            return k * dv + dk * v + dk * dv

        du0, du1 = product(first), product(second)
        inverse = jnp.exp(decay[...])
        come = (du0 + du1 * inverse) * inverse
        whole = jnp.exp(-decay[...] * float(ROWS))
        e_out[...] += whole * come

        def state_copy(j):
            return pltpu.make_async_remote_copy(
                src_ref=e_out, dst_ref=e_in.at[chip], send_sem=es.at[j], recv_sem=er.at[chip],
                device_id={"ctx": 2 * j + core}, device_id_type=MESH,
            )

        for j in range(1, NC // 2):

            @pl.when(j > chip)
            def _():
                state_copy(j).start()

        inside(3)
        qs[0, pl.ds(0, 1), :] += first[0][1]
        qs[1, pl.ds(0, 1), :] += second[0][1]
        early = jnp.sum(modal[...] * inverse, axis=0, keepdims=True)
        conv[0, pl.ds(0, 1), :] += skip[...] * du0 - early * du1
        conv[1, pl.ds(0, 1), :] += skip[...] * du1
        double = whole * whole

        def arrive(i, total):
            pltpu.make_async_remote_copy(
                src_ref=e_out, dst_ref=e_in.at[i], send_sem=es.at[0], recv_sem=er.at[i],
                device_id={"ctx": c + sgn}, device_id_type=MESH,
            ).wait_recv()
            return total * double + e_in[i]

        same = lax.fori_loop(0, chip, arrive, jnp.zeros((MODES, WIDTH), f32))
        s_out[...] = jnp.where(core == 0, whole * (whole * same) + e_out[...], same)
        swap = pltpu.make_async_remote_copy(
            src_ref=s_out, dst_ref=s_in, send_sem=ssem.at[0], recv_sem=ssem.at[1],
            device_id={"ctx": c + sgn}, device_id_type=MESH,
        )
        swap.start()
        rise = modal[...] * mode_a[...]
        swap.wait_recv()
        inward = whole * same + s_in[...] + come
        begin = tuple(
            (ends[n] + inward[n : n + 1, :] * mode_p[n]) * rise[n : n + 1, :] for n in range(MODES)
        )

        def spread(t, state):
            total = conv[t]
            for n in range(MODES):
                total = total + state[n]
            gated = qs[t] * total
            for k in range(2):
                gate[k, pl.ds(t, CHUNKS, stride=SPAN), :] = gated[:, k * 128 : (k + 1) * 128]
            return tuple(state[n] * mode_b[n] for n in range(MODES))

        lax.fori_loop(0, SPAN, spread, begin, unroll=UN)
        for k in range(2):
            cols = pl.ds(k * 128, 128)
            g2[h, :, cols] = (g1[h, :, cols].astype(f32) + gate[k]).astype(bf16)

    if STOP >= 4:
        out_copy = pltpu.make_async_copy(g2.at[h], mixed, osem)
        out_copy.start()

        def kv_copy(src, org, n, sem, to):
            return pltpu.make_async_remote_copy(
                src_ref=src, dst_ref=kvs.at[org, n], send_sem=sem, recv_sem=kr.at[org, n],
                device_id={"ctx": to}, device_id_type=MESH,
            )

        sibling = c + sgn

        half = NC // 4

        def kv_goes(j, n):
            if j < half or not TREE[n]:
                return j > chip
            return jnp.logical_or(j == chip + half, jnp.logical_and(j > chip, chip >= half))

        def relay_copy(j, n):
            org = c - 2 * half
            return kv_copy(kvs.at[org, n], org, n, rs.at[j - half, n], 2 * j + core)

        def relay(n):
            @pl.when(jnp.logical_and(chip >= half, TREE[n] == 1))
            def _():
                relay_copy(half, n).wait_recv()
                for j in range(half, 2 * half):

                    @pl.when(j != chip)
                    def _():
                        relay_copy(j, n).start()

        def finish(n):
            lo = n * GROUP
            here = pl.ds(lo, GROUP)
            rows = acc2[here, :] * row_scale(lo, GROUP)
            cosine, sine = cs[here, pl.ds(0, HD)], cs[here, pl.ds(HD, HD)]

            def turn(x):
                return x * cosine + pltpu.roll(x, HD // 2, 1) * sine

            kv[n, :, pl.ds(0, HD)] = turn(rows[:, HD : 2 * HD]).astype(bf16)
            kv[n, :, pl.ds(HD, HD)] = rows[:, 2 * HD :].T.astype(bf16)
            if STOP >= 5:
                for k in range(1, NC // 2):
                    j = NC // 2 - k if DESC else k

                    @pl.when(kv_goes(j, n))
                    def _(j=j):
                        kv_copy(kv.at[n], c, n, ks.at[j, n], 2 * j + core).start()

                @pl.when(core == 0)
                def _():
                    kv_copy(kv.at[n], c, n, ks.at[0, n], sibling).start()

            qt[:, here] = turn(rows[:, :HD]).T.astype(bf16)

        def before_second():
            sq[...] = jnp.zeros_like(sq)
            acc2[...] = jnp.zeros_like(acc2)
            for copy in wcopies[3:]:
                copy.wait()

        def finished(n):
            if len(PARTS2) > 1:
                finish(n)
            else:
                finish(0)
                finish(1)

            if STOP >= 5 and n == 1:
                relay(0)

        gather(g2, 1, PARTS2, before_second, folder(g2, again, w2s, acc2), finished)

    if STOP >= 5:
        factor = 1.0 / HD**0.5

        def attend(refs, diagonal):
            keys = jnp.concatenate([ref[:, pl.ds(0, HD)] for ref in refs], axis=0)
            scores = jnp.dot(keys, qt[...], preferred_element_type=f32) * factor
            if diagonal:
                key = lax.broadcasted_iota(jnp.int32, scores.shape, 0)
                query = lax.broadcasted_iota(jnp.int32, scores.shape, 1)
                scores = jnp.where(key <= query, scores, -1e30)
            best = jnp.max(scores, axis=0, keepdims=True)
            if not diagonal:
                best = jnp.maximum(best, m_s[...])
            weights = jnp.exp(scores - best)
            sums = jnp.sum(weights, axis=0, keepdims=True)
            values = jnp.concatenate([ref[:, pl.ds(HD, HD)] for ref in refs], axis=1)
            update = jnp.dot(values, weights.astype(bf16), preferred_element_type=f32)
            if diagonal:
                l_s[...] = sums
                o_s[...] = update
            else:
                rescale = jnp.exp(m_s[...] - best)
                l_s[...] = l_s[...] * rescale + sums
                o_s[...] = o_s[...] * rescale + update
            m_s[...] = best

        def origin(k):
            return 2 * (chip - 1 - k) + core

        def pass_on(k, n):
            org = origin(k)

            @pl.when(jnp.logical_or(org != c - 2 * half, TREE[n] == 0))
            def _():
                kv_copy(kv.at[n], org, n, ks.at[0, n], sibling).wait_recv()

            kv_copy(kvs.at[org, n], org, n, fs.at[k, n], sibling).start()

        def both_cores(k, n):
            org = origin(k)
            other = org + sgn
            kv_copy(kv.at[n], other, n, ks.at[0, n], sibling).wait_recv()
            if not NOATT:
                attend((kvs.at[org, n], kvs.at[other, n]), False)

        attend((kv.at[0], kv.at[1]), True)
        relay(1)

        @pl.when(core == 1)
        def _():
            for n in range(2):
                kv_copy(kv.at[n], c - 1, n, ks.at[0, n], 0).wait_recv()
            attend((kvs.at[c - 1, 0], kvs.at[c - 1, 1]), False)

        for n in range(2):
            lag = (LAG0, LAG1)[n]

            def lagged(k, _):
                @pl.when(k < chip)
                def _():
                    pass_on(k, n)

                @pl.when(k >= lag)
                def _():
                    both_cores(k - lag, n)

                return 0

            lax.fori_loop(0, jnp.where(chip > 0, chip + lag, 0), lagged, 0)

        att[...] = (o_s[...] / l_s[...]).T.astype(bf16)
        att_copy = pltpu.make_async_copy(att, attended, asem)
        att_copy.start()

    if STOP < 4:
        for copy in wcopies[3:]:
            copy.wait()
    if STOP >= 1:
        sent(g1, 0, PARTS1)
    if STOP >= 4:
        sent(g2, 1, PARTS2)
        out_copy.wait()
    if STOP >= 5:
        att_copy.wait()
    if STOP >= 2:
        halo.wait_send()
    if STOP == 2:
        halo.wait_recv()
    if STOP >= 3:
        swap.wait_send()
        for j in range(1, NC // 2):

            @pl.when(j > chip)
            def _():
                state_copy(j).wait_send()

    if STOP >= 5:
        for n in range(2):

            @pl.when(core == 0)
            def _():
                kv_copy(kv.at[n], c, n, ks.at[0, n], sibling).wait_send()

            for j in range(1, NC // 2):

                @pl.when(kv_goes(j, n))
                def _():
                    kv_copy(kv.at[n], c, n, ks.at[j, n], 2 * j + core).wait_send()

            for j in range(half, 2 * half):

                @pl.when(jnp.logical_and(chip >= half, j != chip) if TREE[n] else False)
                def _():
                    relay_copy(j, n).wait_send()

            def passed(k, _):
                org = origin(k)
                kv_copy(kvs.at[org, n], org, n, fs.at[k, n], sibling).wait_send()
                return 0

            lax.fori_loop(0, chip, passed, 0)


def local(residual, hyena_gain, in_weight, short_filter, decay_rate, residue, skip_gain, attn_gain, qkv_weight):
    far, near = rope_tables()
    vmem = pl.BlockSpec(memory_space=pltpu.VMEM)
    hbm = pl.BlockSpec(memory_space=pltpu.MemorySpace.HBM)
    dma = pltpu.SemaphoreType.DMA
    return pl.pallas_call(
        kernel,
        out_shape=(
            jax.ShapeDtypeStruct((ROWS, WIDTH), bf16),
            jax.ShapeDtypeStruct((ROWS, HD), bf16),
        ),
        in_specs=[hbm] * 11,
        out_specs=(hbm, hbm),
        scratch_shapes=[
            pltpu.VMEM((1, NH * WIDTH), f32),
            pltpu.VMEM((3, 3, WIDTH), f32),
            pltpu.VMEM((MODES, WIDTH), f32),
            pltpu.VMEM((MODES, WIDTH), f32),
            pltpu.VMEM((1, WIDTH), f32),
            pltpu.VMEM((1, NH * WIDTH), f32),
            pltpu.VMEM((NC, 1, 2 * HD), f32),
            pltpu.VMEM((ROWS, 2 * HD), f32),
            pltpu.VMEM((NH, ROWS, WIDTH), bf16),
            pltpu.VMEM((NH, ROWS, WIDTH), bf16),
            pltpu.VMEM((NH * WIDTH, 3 * WIDTH), bf16),
            pltpu.VMEM((NH * WIDTH, 3 * HD), bf16),
            pltpu.VMEM((ROWS, 3 * WIDTH), f32),
            pltpu.VMEM((ROWS, 3 * HD), f32),
            pltpu.VMEM((ROWS, 128), f32),
            pltpu.VMEM((6, ROWS + 8, 128), f32),
            pltpu.VMEM((16, 3 * WIDTH), bf16),
            pltpu.VMEM((16, 3 * WIDTH), bf16),
            pltpu.VMEM((MODES, WIDTH), f32),
            pltpu.VMEM((MODES, CHUNKS, WIDTH), f32),
            pltpu.VMEM((MODES, CHUNKS, WIDTH), f32),
            pltpu.VMEM((SPAN, CHUNKS, WIDTH), f32),
            pltpu.VMEM((MODES, WIDTH), f32),
            pltpu.VMEM((2 * SPAN, CHUNKS, WIDTH), f32),
            pltpu.VMEM((SPAN, CHUNKS, WIDTH), f32),
            pltpu.VMEM((SPAN, CHUNKS, WIDTH), f32),
            pltpu.VMEM((MODES, CHUNKS, WIDTH), f32),
            pltpu.VMEM((2, ROWS, 128), f32),
            pltpu.VMEM((MODES, WIDTH), f32),
            pltpu.VMEM((NC // 2, MODES, WIDTH), f32),
            pltpu.VMEM((MODES, WIDTH), f32),
            pltpu.VMEM((MODES, WIDTH), f32),
            pltpu.VMEM((ROWS, 2 * HD), f32),
            pltpu.VMEM((HD, ROWS), bf16),
            pltpu.VMEM((2, GROUP, 2 * HD), bf16),
            pltpu.VMEM((NC, 2, GROUP, 2 * HD), bf16),
            pltpu.VMEM((1, ROWS), f32),
            pltpu.VMEM((1, ROWS), f32),
            pltpu.VMEM((HD, ROWS), f32),
            pltpu.VMEM((ROWS, HD), bf16),
            dma((9,)),
            dma,
            dma,
            dma((6,)),
            dma((2, 8)),
            dma((2, 8, NH)),
            dma((2,)),
            dma((2,)),
            dma((NC,)),
            dma((NC,)),
            dma((NC // 2, 2)),
            dma((NC, 2)),
            dma((NC // 2, 2)),
            dma((NC // 4, 2)),
        ],
        compiler_params=pltpu.CompilerParams(
            collective_id=1, has_side_effects=True, vmem_limit_bytes=56 << 20
        ),
        name="genome",
    )(
        residual,
        hyena_gain.reshape(1, -1),
        in_weight.transpose(1, 0, 2),
        short_filter,
        decay_rate.T,
        residue.T,
        skip_gain.reshape(1, -1),
        attn_gain.reshape(1, -1),
        qkv_weight.transpose(1, 0, 2),
        far.reshape(NC, 1, -1),
        near,
    )


def solution(mesh):
    return jax.shard_map(
        local,
        mesh=mesh,
        in_specs=(
            P("ctx", "head"),
            P(),
            P(None, None, "head"),
            P(None, None, "head"),
            P("head", None),
            P("head", None),
            P("head"),
            P(),
            P(None, None, "head"),
        ),
        out_specs=(P("ctx", "head"), P("ctx", "head")),
        check_vma=False,
    )
```

```python
import functools

import jax
import jax.numpy as jnp
import numpy as np
from jax import lax
from jax.experimental import pallas as pl
from jax.experimental.pallas import tpu as pltpu
from jax.sharding import PartitionSpec as P

MESH = pl.DeviceIdType.MESH
f32 = jnp.float32
bf16 = jnp.bfloat16

HD = 128
EPS = 1e-6
ROWS = 256
WIDTH = 256
NH = 16
NC = 16
NZ = 8
MODES = 16
SPAN = 32
CHUNKS = 8
STOP = 9
NOATT = 0
TREE = (0, 1)
DESC = 1
UN = 4
LAG0 = 8
LAG1 = 3
NOFOLD = 0
DIST = 4
PARTS1 = (((0, 80, 0), (80, 48, 1), (128, 80, 0), (208, 48, 1)),)
PARTS2 = (((0, 80, 0), (80, 48, 1)), ((128, 80, 0), (208, 48, 1)))
GROUP = 128
KVORDER = 1


def rope_tables():
    half = HD // 2
    inverse = 10000.0 ** (-np.arange(half) / half)

    def table(positions):
        angle = positions[:, None] * inverse[None, :]
        cos, sin = np.cos(angle), np.sin(angle)
        return np.concatenate([cos, cos, sin, sin], axis=1).astype(np.float32)

    return table(np.arange(NC) * float(ROWS)), table(np.arange(ROWS) * 1.0)


def kernel(
    res_h, hgain_h, w1, taps_h, decay_h, residue_h, skip_h, again_h, w2, far_h, near_h,
    mixed, attended,
    hgain, taps, decay, residue, skip, again, far, near,
    g1, g2, w1s, w2s, acc1, acc2, sq, strm, halo_out, halo_in,
    mode_a, mode_b, mode_p, mode_f, modal, upad, qs, conv, ends, gate, e_out, e_in, s_out, s_in,
    cs, qt, kv, kvs, m_s, l_s, o_s, att,
    psem, osem, asem, wsem, gs, gr, hsem, ssem, es, er, ks, kr, fs, rs,
):
    c = lax.axis_index("ctx")
    h = lax.axis_index("head")
    core = lax.rem(c, 2)
    sgn = 1 - 2 * core
    z = lax.rem(h, NZ)
    xh = h // NZ
    chip = c // 2

    def head(x, zz):
        return x * NZ + lax.rem(zz + 2 * NZ, NZ)

    partner = head(1 - xh, z)
    ahead = head(xh, z + sgn)
    behind = head(xh, z - sgn)

    small = ((res_h, g1.at[h]), (decay_h, decay), (residue_h, residue), (skip_h, skip), (hgain_h, hgain),
             (taps_h, taps), (far_h, far), (near_h, near), (again_h, again))
    scopies = [pltpu.make_async_copy(a, b, psem.at[k]) for k, (a, b) in enumerate(small)]
    for copy in scopies:
        copy.start()
    wcopies = []
    for j in range(3):
        wcopies.append(pltpu.make_async_copy(w1.at[j], w1s.at[:, pl.ds(j * WIDTH, WIDTH)], wsem.at[j]))
    for j in range(3):
        wcopies.append(pltpu.make_async_copy(w2.at[j], w2s.at[:, pl.ds(j * HD, HD)], wsem.at[3 + j]))
    for copy in wcopies:
        copy.start()

    barrier = pltpu.get_barrier_semaphore()
    slant, slant_back = head(1 - xh, z + sgn), head(1 - xh, z - sgn)
    for to in (partner, ahead, behind, slant, slant_back):
        pl.semaphore_signal(barrier, inc=1, device_id={"head": to}, device_id_type=MESH)
    for k in range(1, NC // 2):
        to = 2 * lax.rem(chip + k, NC // 2) + core
        pl.semaphore_signal(barrier, inc=1, device_id={"ctx": to}, device_id_type=MESH)
    for k in (1, NC - 1):
        pl.semaphore_signal(
            barrier, inc=1, device_id={"ctx": lax.rem(c + k, NC)}, device_id_type=MESH
        )
    pl.semaphore_wait(barrier, 5 + NC // 2 - 1 + 2)
    scopies[0].wait()


    def gather(g, which, groups, prepare, fold, done):
        numbers, count = [], 0
        for group in groups:
            numbers.append(range(count, count + len(group)))
            count += len(group)
        flat = [part for group in groups for part in group]

        def copy(p, org, to):
            rows = g.at[org, pl.ds(flat[p][0], flat[p][1])]
            return pltpu.make_async_remote_copy(
                src_ref=rows, dst_ref=rows, send_sem=gs.at[which, p], recv_sem=gr.at[which, p, org],
                device_id={"head": to}, device_id_type=MESH,
            )

        def send(p, org, to):
            copy(p, org, to).start()

        def wait(p, org):
            copy(p, org, partner).wait_recv()

        def begin(n):
            for p in numbers[n]:
                if flat[p][2]:
                    send(p, h, slant)
                    send(p, h, slant_back)
            for p in numbers[n]:
                send(p, h, ahead)
                send(p, h, behind)
            for p in numbers[n]:
                send(p, h, partner)

        def step(n, d, between=lambda j: None):
            a, b = head(xh, z - sgn * d), head(xh, z + sgn * d)
            a2, b2 = head(1 - xh, z - sgn * d), head(1 - xh, z + sgn * d)

            def hop(p, org, to, far, over):
                wait(p, org)

                @pl.when(d < far)
                def _():
                    send(p, org, to)
                    if over and far == 3:
                        send(p, org, partner)

                if over and far == 3:

                    @pl.when(d == 3)
                    def _():
                        send(p, org, partner)

                if over and far == 4:

                    @pl.when(d == 3)
                    def _():
                        send(p, org, slant)

                    @pl.when(d < 4)
                    def _():
                        send(p, org, partner)

            def both(p, first, second, to, back, over):
                hop(p, first, to, 4, over)

                @pl.when(d < 4)
                def _():
                    hop(p, second, back, 3, over)

            calls = [(p, a, b, ahead, behind, not flat[p][2]) for p in numbers[n]]
            calls += [(p, b2, a2, behind, ahead, False) for p in numbers[n] if flat[p][2]]
            for i, call in enumerate(calls):
                both(*call)
                for j in range(4 * i // len(calls), 4 * (i + 1) // len(calls)):
                    between(j)

        def folds(n, d):
            def one(j):
                over = j >= jnp.where(d == 1, 3, jnp.where(d == 4, 1, 2))
                here = jnp.where(d == 1, j, 2 * d - 1 + j)
                there = jnp.where(d == 1, 0, jnp.where(d == 4, 4 + j, 2 * d - 5 + j))
                k = jnp.where(over, there, here)
                apart = jnp.where(k % 2 == 1, -((k + 1) // 2), k // 2)
                org = head(jnp.where(over, 1 - xh, xh), z + sgn * apart)

                @pl.when(over)
                def _():
                    for p in numbers[n]:
                        if not flat[p][2]:
                            wait(p, org)

                @pl.when(jnp.logical_and(over, k == 0))
                def _():
                    for p in numbers[n]:
                        if flat[p][2]:
                            wait(p, org)

                if not NOFOLD:
                    fold(groups[n], org)

            return one

        def some_folds(n, d, lo, hi):
            one = folds(n, d)

            def body(j, _):
                one(j)
                return 0

            lax.fori_loop(lo, hi, body, 0)

        def final(n):
            a, b2 = head(xh, z + 4), head(1 - xh, z + 4)
            for p in numbers[n]:
                wait(p, a)
            some_folds(n, 3, 0, 4)
            some_folds(n, 4, 0, 3)
            for p in numbers[n]:
                if flat[p][2]:
                    wait(p, b2)
            some_folds(n, 4, 3, 4)
            done(n)

        lag = len(groups) > 1
        for n in range(len(groups)):
            begin(n)
        step(0, 1)
        prepare()

        def later(d, _):
            step(0, d, folds(0, d - 1))
            if lag:
                step(1, d - 1)

                @pl.when(d > 2)
                def _():
                    some_folds(1, d - 2, 0, 4)

            return 0

        lax.fori_loop(2, 4, later, 0)
        if lag:
            step(1, 3)
        final(0)
        if lag:
            some_folds(1, 2, 0, 4)
            final(1)

    def sent(g, which, groups):
        for p, part in enumerate(part for group in groups for part in group):
            rows = g.at[pl.ds(0, NH - 1), pl.ds(part[0], part[1])]
            pltpu.make_async_remote_copy(
                src_ref=rows, dst_ref=rows, send_sem=gs.at[which, p], recv_sem=gr.at[which, p, 0],
                device_id={"head": partner}, device_id_type=MESH,
            ).wait_send()

    def folder(g, gain, w, acc):
        def fold(group, org):
            lo, n = group[0][0], sum(part[1] for part in group)
            here = pl.ds(lo, n)
            columns = pl.ds(pl.multiple_of(org * WIDTH, WIDTH), WIDTH)
            rows = g[org, here].astype(f32)
            squares = rows * rows
            sq[here, :] += squares[:, :128] + squares[:, 128:]
            scaled = (rows * gain[:, columns]).astype(bf16)
            acc[here, :] += jnp.dot(scaled, w[columns, :], preferred_element_type=f32)

        return fold

    def row_scale(lo, n):
        total = jnp.sum(sq[pl.ds(lo, n), :], axis=1, keepdims=True)
        return lax.rsqrt(total * (1.0 / (NH * WIDTH)) + EPS)

    def tables():
        d = decay[...]
        a = jnp.exp(-d)
        mode_a[...] = a
        twice = 2.0 * d
        series = twice * (1.0 - twice * (0.5 - twice * (1.0 / 6 - twice * (1.0 / 24 - twice * (1.0 / 120)))))
        coef = residue[...] * jnp.sqrt(jnp.where(twice < 0.1, series, 1.0 - jnp.exp(-twice)))
        modal[...] = coef
        steps = lax.broadcasted_iota(jnp.int32, (CHUNKS, WIDTH), 0).astype(f32)
        for n in range(MODES):
            mode_b[n] = jnp.broadcast_to(mode_a[pl.ds(n, 1), :], (CHUNKS, WIDTH))
            mode_p[n] = jnp.exp(-decay[pl.ds(n, 1), :] * (steps * SPAN))
        lags = lax.broadcasted_iota(jnp.int32, (SPAN, WIDTH), 0).astype(f32)
        filt = jnp.zeros((SPAN, WIDTH), f32)
        for n in range(MODES):
            filt = filt + modal[pl.ds(n, 1), :] * jnp.exp(-decay[pl.ds(n, 1), :] * lags)
        filt = filt + jnp.where(lags == 0.0, skip[...], 0.0)
        for t in range(SPAN):
            mode_f[t] = jnp.broadcast_to(filt[t : t + 1, :], (CHUNKS, WIDTH))
        upad[pl.ds(0, SPAN)] = jnp.zeros((SPAN, CHUNKS, WIDTH), f32)
        there = far[c]
        fc, fsn = there[:, :HD], there[:, HD:]
        nc, ns = near[:, pl.ds(0, HD)], near[:, pl.ds(HD, HD)]
        cs[:, pl.ds(0, HD)] = nc * fc - ns * fsn
        lane = lax.broadcasted_iota(jnp.int32, (ROWS, HD), 1)
        sine = ns * fc + nc * fsn
        cs[:, pl.ds(HD, HD)] = jnp.where(lane < HD // 2, -sine, sine)

    def before_first():
        for copy in scopies[1:]:
            copy.wait()
        tables()
        sq[...] = jnp.zeros_like(sq)
        acc1[...] = jnp.zeros_like(acc1)
        for copy in wcopies[:3]:
            copy.wait()

    if STOP < 1:
        before_first()
    if STOP >= 1:
        gather(g1, 0, PARTS1, before_first, folder(g1, hgain, w1s, acc1), lambda n: None)

    if STOP >= 2:
        last = ROWS - 16
        halo_out[...] = (acc1[pl.ds(last, 16), :] * row_scale(last, 16)).astype(bf16)
        halo = pltpu.make_async_remote_copy(
            src_ref=halo_out, dst_ref=halo_in, send_sem=hsem.at[0], recv_sem=hsem.at[1],
            device_id={"ctx": lax.rem(c + 1, NC)}, device_id_type=MESH,
        )
        halo.start()
        for k in range(6):
            strm[k, pl.ds(0, 8), :] = jnp.zeros((8, 128), f32)

        def to_streams(i, _):
            lo = pl.multiple_of(i * 32, 32)
            block = (acc1[pl.ds(lo, 32), :] * row_scale(lo, 32)).astype(bf16)
            block = block.astype(f32)
            for k in range(6):
                strm[k, pl.ds(lo + 8, 32), :] = block[:, k * 128 : (k + 1) * 128]
            return 0

        lax.fori_loop(0, ROWS // 32, to_streams, 0)

        def tap(j, s):
            return taps[j, pl.ds(s, 1), :]

        def stream_rows(start):
            return jnp.concatenate(
                [strm[k, pl.ds(start, CHUNKS, stride=SPAN), :] for k in range(6)], axis=1
            )

        def short(now, one, two):
            out = []
            for s in range(3):
                cols = slice(s * WIDTH, (s + 1) * WIDTH)
                out.append(tap(0, s) * now[:, cols] + tap(1, s) * one[:, cols] + tap(2, s) * two[:, cols])
            return out

        def short_step(s, rows):
            one, two = rows
            now = stream_rows(s + 8)
            q, k, v = short(now, one, two)
            qs[s] = q
            upad[SPAN + s] = k * v
            return now, one

        lax.fori_loop(0, SPAN, short_step, (stream_rows(7), stream_rows(6)), unroll=UN)

    if STOP >= 3:
        def horner(s, state):
            u = upad[SPAN + s]
            return tuple(state[n] * mode_b[n] + u for n in range(MODES))

        zero = jnp.zeros((CHUNKS, WIDTH), f32)
        state = lax.fori_loop(0, SPAN, horner, (zero,) * MODES, unroll=UN)
        sub = lax.broadcasted_iota(jnp.int32, (CHUNKS, WIDTH), 0)
        for n in range(MODES):
            e = state[n]
            for k in (1, 2, 4):
                moved = jnp.where(sub >= k, pltpu.roll(e, k, 0), 0.0)
                e = e + mode_p[n, pl.ds(k, 1), :] * moved
            e_out[pl.ds(n, 1), :] = e[CHUNKS - 1 : CHUNKS, :]
            ends[n] = jnp.where(sub >= 1, pltpu.roll(e, 1, 0), 0.0)

        def inside(block):
            def lag(d, total):
                return total + mode_f[d][None] * upad[pl.ds(SPAN + block * 8 - d, 8)]

            conv[pl.ds(block * 8, 8)] = lax.fori_loop(
                0, block * 8 + 8, lag, jnp.zeros((8, CHUNKS, WIDTH), f32), unroll=UN
            )

        for block in range(3):
            inside(block)

        halo.wait_recv()
        before = jnp.where(c == 0, 0.0, halo_in[...].astype(f32)[14:16, :])
        first, second = [], []
        for s in range(3):
            two, one = (before[r : r + 1, s * WIDTH : (s + 1) * WIDTH] for r in range(2))
            now, then = (
                jnp.concatenate([strm[2 * s + k, pl.ds(8 + r, 1), :] for k in range(2)], axis=1)
                for r in range(2)
            )
            base = tap(0, s) * now
            first.append((base, tap(1, s) * one + tap(2, s) * two))
            base = tap(0, s) * then + tap(1, s) * now
            second.append((base, tap(2, s) * one))

        def product(pair):
            (k, dk), (v, dv) = pair[1:]
            return k * dv + dk * v + dk * dv

        du0, du1 = product(first), product(second)
        inverse = jnp.exp(decay[...])
        come = (du0 + du1 * inverse) * inverse
        whole = jnp.exp(-decay[...] * float(ROWS))
        e_out[...] += whole * come

        def state_copy(j):
            return pltpu.make_async_remote_copy(
                src_ref=e_out, dst_ref=e_in.at[chip], send_sem=es.at[j], recv_sem=er.at[chip],
                device_id={"ctx": 2 * j + core}, device_id_type=MESH,
            )

        for j in range(1, NC // 2):

            @pl.when(j > chip)
            def _():
                state_copy(j).start()

        inside(3)
        qs[0, pl.ds(0, 1), :] += first[0][1]
        qs[1, pl.ds(0, 1), :] += second[0][1]
        early = jnp.sum(modal[...] * inverse, axis=0, keepdims=True)
        conv[0, pl.ds(0, 1), :] += skip[...] * du0 - early * du1
        conv[1, pl.ds(0, 1), :] += skip[...] * du1
        double = whole * whole

        def arrive(i, total):
            pltpu.make_async_remote_copy(
                src_ref=e_out, dst_ref=e_in.at[i], send_sem=es.at[0], recv_sem=er.at[i],
                device_id={"ctx": c + sgn}, device_id_type=MESH,
            ).wait_recv()
            return total * double + e_in[i]

        same = lax.fori_loop(0, chip, arrive, jnp.zeros((MODES, WIDTH), f32))
        s_out[...] = jnp.where(core == 0, whole * (whole * same) + e_out[...], same)
        swap = pltpu.make_async_remote_copy(
            src_ref=s_out, dst_ref=s_in, send_sem=ssem.at[0], recv_sem=ssem.at[1],
            device_id={"ctx": c + sgn}, device_id_type=MESH,
        )
        swap.start()
        rise = modal[...] * mode_a[...]
        swap.wait_recv()
        inward = whole * same + s_in[...] + come
        begin = tuple(
            (ends[n] + inward[n : n + 1, :] * mode_p[n]) * rise[n : n + 1, :] for n in range(MODES)
        )

        def spread(t, state):
            total = conv[t]
            for n in range(MODES):
                total = total + state[n]
            gated = qs[t] * total
            for k in range(2):
                gate[k, pl.ds(t, CHUNKS, stride=SPAN), :] = gated[:, k * 128 : (k + 1) * 128]
            return tuple(state[n] * mode_b[n] for n in range(MODES))

        lax.fori_loop(0, SPAN, spread, begin, unroll=UN)
        for k in range(2):
            cols = pl.ds(k * 128, 128)
            g2[h, :, cols] = (g1[h, :, cols].astype(f32) + gate[k]).astype(bf16)

    if STOP >= 4:
        out_copy = pltpu.make_async_copy(g2.at[h], mixed, osem)
        out_copy.start()

        def kv_copy(src, org, n, sem, to):
            return pltpu.make_async_remote_copy(
                src_ref=src, dst_ref=kvs.at[org, n], send_sem=sem, recv_sem=kr.at[org, n],
                device_id={"ctx": to}, device_id_type=MESH,
            )

        sibling = c + sgn

        half = NC // 4

        def kv_goes(j, n):
            if j < half or not TREE[n]:
                return j > chip
            return jnp.logical_or(j == chip + half, jnp.logical_and(j > chip, chip >= half))

        def relay_copy(j, n):
            org = c - 2 * half
            return kv_copy(kvs.at[org, n], org, n, rs.at[j - half, n], 2 * j + core)

        def relay(n):
            @pl.when(jnp.logical_and(chip >= half, TREE[n] == 1))
            def _():
                relay_copy(half, n).wait_recv()
                for j in range(half, 2 * half):

                    @pl.when(j != chip)
                    def _():
                        relay_copy(j, n).start()

        def finish(n):
            lo = n * GROUP
            here = pl.ds(lo, GROUP)
            rows = acc2[here, :] * row_scale(lo, GROUP)
            cosine, sine = cs[here, pl.ds(0, HD)], cs[here, pl.ds(HD, HD)]

            def turn(x):
                return x * cosine + pltpu.roll(x, HD // 2, 1) * sine

            kv[n, :, pl.ds(0, HD)] = turn(rows[:, HD : 2 * HD]).astype(bf16)
            kv[n, :, pl.ds(HD, HD)] = rows[:, 2 * HD :].T.astype(bf16)
            if STOP >= 5:
                for k in range(1, NC // 2):
                    j = NC // 2 - k if DESC else k

                    @pl.when(kv_goes(j, n))
                    def _(j=j):
                        kv_copy(kv.at[n], c, n, ks.at[j, n], 2 * j + core).start()

                @pl.when(core == 0)
                def _():
                    kv_copy(kv.at[n], c, n, ks.at[0, n], sibling).start()

            qt[:, here] = turn(rows[:, :HD]).T.astype(bf16)

        def before_second():
            sq[...] = jnp.zeros_like(sq)
            acc2[...] = jnp.zeros_like(acc2)
            for copy in wcopies[3:]:
                copy.wait()

        def finished(n):
            if len(PARTS2) > 1:
                finish(n)
            else:
                finish(0)
                finish(1)

            if STOP >= 5 and n == 1:
                relay(0)

        gather(g2, 1, PARTS2, before_second, folder(g2, again, w2s, acc2), finished)

    def settle():
        if STOP >= 1:
            sent(g1, 0, PARTS1)
        if STOP >= 2:
            halo.wait_send()
        if STOP == 2:
            halo.wait_recv()
        if STOP >= 3:
            swap.wait_send()
            for j in range(1, NC // 2):

                @pl.when(j > chip)
                def _():
                    state_copy(j).wait_send()

        if STOP >= 4:
            sent(g2, 1, PARTS2)
            out_copy.wait()
        if STOP >= 5:
            for n in range(2):

                @pl.when(core == 0)
                def _():
                    kv_copy(kv.at[n], c, n, ks.at[0, n], sibling).wait_send()

                for j in range(1, NC // 2):

                    @pl.when(kv_goes(j, n))
                    def _():
                        kv_copy(kv.at[n], c, n, ks.at[j, n], 2 * j + core).wait_send()

    if STOP >= 5:
        factor = 1.0 / HD**0.5

        def attend(refs, diagonal):
            keys = jnp.concatenate([ref[:, pl.ds(0, HD)] for ref in refs], axis=0)
            scores = jnp.dot(keys, qt[...], preferred_element_type=f32) * factor
            if diagonal:
                key = lax.broadcasted_iota(jnp.int32, scores.shape, 0)
                query = lax.broadcasted_iota(jnp.int32, scores.shape, 1)
                scores = jnp.where(key <= query, scores, -1e30)
            best = jnp.max(scores, axis=0, keepdims=True)
            if not diagonal:
                best = jnp.maximum(best, m_s[...])
            weights = jnp.exp(scores - best)
            sums = jnp.sum(weights, axis=0, keepdims=True)
            values = jnp.concatenate([ref[:, pl.ds(HD, HD)] for ref in refs], axis=1)
            update = jnp.dot(values, weights.astype(bf16), preferred_element_type=f32)
            if diagonal:
                l_s[...] = sums
                o_s[...] = update
            else:
                rescale = jnp.exp(m_s[...] - best)
                l_s[...] = l_s[...] * rescale + sums
                o_s[...] = o_s[...] * rescale + update
            m_s[...] = best

        def origin(k):
            return 2 * (chip - 1 - k) + core

        def pass_on(k, n):
            org = origin(k)

            @pl.when(jnp.logical_or(org != c - 2 * half, TREE[n] == 0))
            def _():
                kv_copy(kv.at[n], org, n, ks.at[0, n], sibling).wait_recv()

            kv_copy(kvs.at[org, n], org, n, fs.at[k, n], sibling).start()

        def both_cores(k, n):
            org = origin(k)
            other = org + sgn
            kv_copy(kv.at[n], other, n, ks.at[0, n], sibling).wait_recv()
            if not NOATT:
                attend((kvs.at[org, n], kvs.at[other, n]), False)

        attend((kv.at[0], kv.at[1]), True)
        relay(1)

        @pl.when(core == 1)
        def _():
            for n in range(2):
                kv_copy(kv.at[n], c - 1, n, ks.at[0, n], 0).wait_recv()
            attend((kvs.at[c - 1, 0], kvs.at[c - 1, 1]), False)

        for n in range(2):
            if n == 1:
                settle()
            lag = (LAG0, LAG1)[n]

            def lagged(k, _):
                @pl.when(k < chip)
                def _():
                    pass_on(k, n)

                @pl.when(k >= lag)
                def _():
                    both_cores(k - lag, n)

                return 0

            lax.fori_loop(0, jnp.where(chip > 0, chip + lag, 0), lagged, 0)

        att[...] = (o_s[...] / l_s[...]).T.astype(bf16)
        att_copy = pltpu.make_async_copy(att, attended, asem)
        att_copy.start()

    if STOP < 5:
        if STOP < 4:
            for copy in wcopies[3:]:
                copy.wait()
        settle()
    if STOP >= 5:
        for n in range(2):
            for j in range(half, 2 * half):

                @pl.when(jnp.logical_and(chip >= half, j != chip) if TREE[n] else False)
                def _():
                    relay_copy(j, n).wait_send()

            def passed(k, _):
                org = origin(k)
                kv_copy(kvs.at[org, n], org, n, fs.at[k, n], sibling).wait_send()
                return 0

            lax.fori_loop(0, chip, passed, 0)
        att_copy.wait()


def write(mixed_in, attended_in, mixed, attended, one, two, sem):
    loads = (
        pltpu.make_async_copy(mixed_in, one, sem.at[0]),
        pltpu.make_async_copy(attended_in, two, sem.at[1]),
    )
    stores = (
        pltpu.make_async_copy(one, mixed, sem.at[2]),
        pltpu.make_async_copy(two, attended, sem.at[3]),
    )
    for copy in loads:
        copy.start()
    for load, store in zip(loads, stores):
        load.wait()
        store.start()
    for copy in stores:
        copy.wait()


def local(residual, hyena_gain, in_weight, short_filter, decay_rate, residue, skip_gain, attn_gain, qkv_weight):
    far, near = rope_tables()
    vmem = pl.BlockSpec(memory_space=pltpu.VMEM)
    hbm = pl.BlockSpec(memory_space=pltpu.MemorySpace.HBM)
    dma = pltpu.SemaphoreType.DMA
    done = pl.pallas_call(
        kernel,
        out_shape=(
            jax.ShapeDtypeStruct((ROWS, WIDTH), bf16),
            jax.ShapeDtypeStruct((ROWS, HD), bf16),
        ),
        in_specs=[hbm] * 11,
        out_specs=(hbm, hbm),
        scratch_shapes=[
            pltpu.VMEM((1, NH * WIDTH), f32),
            pltpu.VMEM((3, 3, WIDTH), f32),
            pltpu.VMEM((MODES, WIDTH), f32),
            pltpu.VMEM((MODES, WIDTH), f32),
            pltpu.VMEM((1, WIDTH), f32),
            pltpu.VMEM((1, NH * WIDTH), f32),
            pltpu.VMEM((NC, 1, 2 * HD), f32),
            pltpu.VMEM((ROWS, 2 * HD), f32),
            pltpu.VMEM((NH, ROWS, WIDTH), bf16),
            pltpu.VMEM((NH, ROWS, WIDTH), bf16),
            pltpu.VMEM((NH * WIDTH, 3 * WIDTH), bf16),
            pltpu.VMEM((NH * WIDTH, 3 * HD), bf16),
            pltpu.VMEM((ROWS, 3 * WIDTH), f32),
            pltpu.VMEM((ROWS, 3 * HD), f32),
            pltpu.VMEM((ROWS, 128), f32),
            pltpu.VMEM((6, ROWS + 8, 128), f32),
            pltpu.VMEM((16, 3 * WIDTH), bf16),
            pltpu.VMEM((16, 3 * WIDTH), bf16),
            pltpu.VMEM((MODES, WIDTH), f32),
            pltpu.VMEM((MODES, CHUNKS, WIDTH), f32),
            pltpu.VMEM((MODES, CHUNKS, WIDTH), f32),
            pltpu.VMEM((SPAN, CHUNKS, WIDTH), f32),
            pltpu.VMEM((MODES, WIDTH), f32),
            pltpu.VMEM((2 * SPAN, CHUNKS, WIDTH), f32),
            pltpu.VMEM((SPAN, CHUNKS, WIDTH), f32),
            pltpu.VMEM((SPAN, CHUNKS, WIDTH), f32),
            pltpu.VMEM((MODES, CHUNKS, WIDTH), f32),
            pltpu.VMEM((2, ROWS, 128), f32),
            pltpu.VMEM((MODES, WIDTH), f32),
            pltpu.VMEM((NC // 2, MODES, WIDTH), f32),
            pltpu.VMEM((MODES, WIDTH), f32),
            pltpu.VMEM((MODES, WIDTH), f32),
            pltpu.VMEM((ROWS, 2 * HD), f32),
            pltpu.VMEM((HD, ROWS), bf16),
            pltpu.VMEM((2, GROUP, 2 * HD), bf16),
            pltpu.VMEM((NC, 2, GROUP, 2 * HD), bf16),
            pltpu.VMEM((1, ROWS), f32),
            pltpu.VMEM((1, ROWS), f32),
            pltpu.VMEM((HD, ROWS), f32),
            pltpu.VMEM((ROWS, HD), bf16),
            dma((9,)),
            dma,
            dma,
            dma((6,)),
            dma((2, 8)),
            dma((2, 8, NH)),
            dma((2,)),
            dma((2,)),
            dma((NC,)),
            dma((NC,)),
            dma((NC // 2, 2)),
            dma((NC, 2)),
            dma((NC // 2, 2)),
            dma((NC // 4, 2)),
        ],
        compiler_params=pltpu.CompilerParams(
            collective_id=1, has_side_effects=True, vmem_limit_bytes=56 << 20
        ),
        name="genome",
    )(
        residual,
        hyena_gain.reshape(1, -1),
        in_weight.transpose(1, 0, 2),
        short_filter,
        decay_rate.T,
        residue.T,
        skip_gain.reshape(1, -1),
        attn_gain.reshape(1, -1),
        qkv_weight.transpose(1, 0, 2),
        far.reshape(NC, 1, -1),
        near,
    )
    return pl.pallas_call(
        write,
        out_shape=(
            jax.ShapeDtypeStruct((ROWS, WIDTH), bf16),
            jax.ShapeDtypeStruct((ROWS, HD), bf16),
        ),
        in_specs=[hbm, hbm],
        out_specs=(hbm, hbm),
        scratch_shapes=[
            pltpu.VMEM((ROWS, WIDTH), bf16),
            pltpu.VMEM((ROWS, HD), bf16),
            dma((4,)),
        ],
        compiler_params=pltpu.CompilerParams(vmem_limit_bytes=56 << 20),
        name="write",
    )(*done)


def solution(mesh):
    return jax.shard_map(
        local,
        mesh=mesh,
        in_specs=(
            P("ctx", "head"),
            P(),
            P(None, None, "head"),
            P(None, None, "head"),
            P("head", None),
            P("head", None),
            P("head"),
            P(),
            P(None, None, "head"),
        ),
        out_specs=(P("ctx", "head"), P("ctx", "head")),
        check_vma=False,
    )
```

```python
import functools

import jax
import jax.numpy as jnp
import numpy as np
from jax import lax
from jax.experimental import pallas as pl
from jax.experimental.pallas import tpu as pltpu
from jax.sharding import PartitionSpec as P

MESH = pl.DeviceIdType.MESH
f32 = jnp.float32
bf16 = jnp.bfloat16

HD = 128
EPS = 1e-6
ROWS = 256
WIDTH = 256
NH = 16
NC = 16
NZ = 8
MODES = 16
SPAN = 32
CHUNKS = 8
STOP = 9
NOATT = 0
TREE = (0, 1)
DESC = 1
UN = 4
LAG0 = 8
LAG1 = 6
NOFOLD = 0
DIST = 4
PARTS1 = (((0, 80, 0), (80, 48, 1), (128, 80, 0), (208, 48, 1)),)
PARTS2 = (((0, 80, 0), (80, 48, 1)), ((128, 80, 0), (208, 48, 1)))
GROUP = 128
KVORDER = 1


def rope_tables():
    half = HD // 2
    inverse = 10000.0 ** (-np.arange(half) / half)

    def table(positions):
        angle = positions[:, None] * inverse[None, :]
        cos, sin = np.cos(angle), np.sin(angle)
        return np.concatenate([cos, cos, sin, sin], axis=1).astype(np.float32)

    return table(np.arange(NC) * float(ROWS)), table(np.arange(ROWS) * 1.0)


def kernel(
    res_h, hgain_h, w1, taps_h, decay_h, residue_h, skip_h, again_h, w2, far_h, near_h,
    mixed, attended,
    hgain, taps, decay, residue, skip, again, far, near,
    g1, g2, w1s, w2s, acc1, acc2, sq, strm, halo_out, halo_in,
    mode_a, mode_b, mode_p, mode_f, modal, upad, qs, conv, ends, gate, e_out, e_in, s_out, s_in,
    cs, qt, kv, kvs, m_s, l_s, o_s, att,
    psem, osem, asem, wsem, gs, gr, hsem, ssem, es, er, ks, kr, fs, rs,
):
    c = lax.axis_index("ctx")
    h = lax.axis_index("head")
    core = lax.rem(c, 2)
    sgn = 1 - 2 * core
    z = lax.rem(h, NZ)
    xh = h // NZ
    chip = c // 2

    def head(x, zz):
        return x * NZ + lax.rem(zz + 2 * NZ, NZ)

    partner = head(1 - xh, z)
    ahead = head(xh, z + sgn)
    behind = head(xh, z - sgn)

    small = ((res_h, g1.at[h]), (decay_h, decay), (residue_h, residue), (skip_h, skip), (hgain_h, hgain),
             (taps_h, taps), (far_h, far), (near_h, near), (again_h, again))
    scopies = [pltpu.make_async_copy(a, b, psem.at[k]) for k, (a, b) in enumerate(small)]
    for copy in scopies:
        copy.start()
    wcopies = []
    for j in range(3):
        wcopies.append(pltpu.make_async_copy(w1.at[j], w1s.at[:, pl.ds(j * WIDTH, WIDTH)], wsem.at[j]))
    for j in range(3):
        wcopies.append(pltpu.make_async_copy(w2.at[j], w2s.at[:, pl.ds(j * HD, HD)], wsem.at[3 + j]))
    for copy in wcopies:
        copy.start()

    barrier = pltpu.get_barrier_semaphore()
    slant, slant_back = head(1 - xh, z + sgn), head(1 - xh, z - sgn)
    for to in (partner, ahead, behind, slant, slant_back):
        pl.semaphore_signal(barrier, inc=1, device_id={"head": to}, device_id_type=MESH)
    for k in range(1, NC // 2):
        to = 2 * lax.rem(chip + k, NC // 2) + core
        pl.semaphore_signal(barrier, inc=1, device_id={"ctx": to}, device_id_type=MESH)
    for k in (1, NC - 1):
        pl.semaphore_signal(
            barrier, inc=1, device_id={"ctx": lax.rem(c + k, NC)}, device_id_type=MESH
        )
    pl.semaphore_wait(barrier, 5 + NC // 2 - 1 + 2)
    scopies[0].wait()


    def gather(g, which, groups, prepare, fold, done):
        numbers, count = [], 0
        for group in groups:
            numbers.append(range(count, count + len(group)))
            count += len(group)
        flat = [part for group in groups for part in group]

        def copy(p, org, to):
            rows = g.at[org, pl.ds(flat[p][0], flat[p][1])]
            return pltpu.make_async_remote_copy(
                src_ref=rows, dst_ref=rows, send_sem=gs.at[which, p], recv_sem=gr.at[which, p, org],
                device_id={"head": to}, device_id_type=MESH,
            )

        def send(p, org, to):
            copy(p, org, to).start()

        def wait(p, org):
            copy(p, org, partner).wait_recv()

        def begin(n):
            for p in numbers[n]:
                if flat[p][2]:
                    send(p, h, slant)
                    send(p, h, slant_back)
            for p in numbers[n]:
                send(p, h, ahead)
                send(p, h, behind)
            for p in numbers[n]:
                send(p, h, partner)

        def step(n, d, between=lambda j: None):
            a, b = head(xh, z - sgn * d), head(xh, z + sgn * d)
            a2, b2 = head(1 - xh, z - sgn * d), head(1 - xh, z + sgn * d)

            def hop(p, org, to, far, over):
                wait(p, org)

                @pl.when(d < far)
                def _():
                    send(p, org, to)
                    if over and far == 3:
                        send(p, org, partner)

                if over and far == 3:

                    @pl.when(d == 3)
                    def _():
                        send(p, org, partner)

                if over and far == 4:

                    @pl.when(d == 3)
                    def _():
                        send(p, org, slant)

                    @pl.when(d < 4)
                    def _():
                        send(p, org, partner)

            def both(p, first, second, to, back, over):
                hop(p, first, to, 4, over)

                @pl.when(d < 4)
                def _():
                    hop(p, second, back, 3, over)

            calls = [(p, a, b, ahead, behind, not flat[p][2]) for p in numbers[n]]
            calls += [(p, b2, a2, behind, ahead, False) for p in numbers[n] if flat[p][2]]
            for i, call in enumerate(calls):
                both(*call)
                for j in range(4 * i // len(calls), 4 * (i + 1) // len(calls)):
                    between(j)

        def folds(n, d):
            def one(j):
                over = j >= jnp.where(d == 1, 3, jnp.where(d == 4, 1, 2))
                here = jnp.where(d == 1, j, 2 * d - 1 + j)
                there = jnp.where(d == 1, 0, jnp.where(d == 4, 4 + j, 2 * d - 5 + j))
                k = jnp.where(over, there, here)
                apart = jnp.where(k % 2 == 1, -((k + 1) // 2), k // 2)
                org = head(jnp.where(over, 1 - xh, xh), z + sgn * apart)

                @pl.when(over)
                def _():
                    for p in numbers[n]:
                        if not flat[p][2]:
                            wait(p, org)

                @pl.when(jnp.logical_and(over, k == 0))
                def _():
                    for p in numbers[n]:
                        if flat[p][2]:
                            wait(p, org)

                if not NOFOLD:
                    fold(groups[n], org)

            return one

        def some_folds(n, d, lo, hi):
            one = folds(n, d)

            def body(j, _):
                one(j)
                return 0

            lax.fori_loop(lo, hi, body, 0)

        def final(n):
            a, b2 = head(xh, z + 4), head(1 - xh, z + 4)
            for p in numbers[n]:
                wait(p, a)
            some_folds(n, 3, 0, 4)
            some_folds(n, 4, 0, 3)
            for p in numbers[n]:
                if flat[p][2]:
                    wait(p, b2)
            some_folds(n, 4, 3, 4)
            done(n)

        lag = len(groups) > 1
        for n in range(len(groups)):
            begin(n)
        step(0, 1)
        prepare()

        def later(d, _):
            step(0, d, folds(0, d - 1))
            if lag:
                step(1, d - 1)

                @pl.when(d > 2)
                def _():
                    some_folds(1, d - 2, 0, 4)

            return 0

        lax.fori_loop(2, 4, later, 0)
        if lag:
            step(1, 3)
        final(0)
        if lag:
            some_folds(1, 2, 0, 4)
            final(1)

    def sent(g, which, groups):
        for p, part in enumerate(part for group in groups for part in group):
            rows = g.at[pl.ds(0, NH - 1), pl.ds(part[0], part[1])]
            pltpu.make_async_remote_copy(
                src_ref=rows, dst_ref=rows, send_sem=gs.at[which, p], recv_sem=gr.at[which, p, 0],
                device_id={"head": partner}, device_id_type=MESH,
            ).wait_send()

    def folder(g, gain, w, acc):
        def fold(group, org):
            lo, n = group[0][0], sum(part[1] for part in group)
            here = pl.ds(lo, n)
            columns = pl.ds(pl.multiple_of(org * WIDTH, WIDTH), WIDTH)
            rows = g[org, here].astype(f32)
            squares = rows * rows
            sq[here, :] += squares[:, :128] + squares[:, 128:]
            scaled = (rows * gain[:, columns]).astype(bf16)
            acc[here, :] += jnp.dot(scaled, w[columns, :], preferred_element_type=f32)

        return fold

    def row_scale(lo, n):
        total = jnp.sum(sq[pl.ds(lo, n), :], axis=1, keepdims=True)
        return lax.rsqrt(total * (1.0 / (NH * WIDTH)) + EPS)

    def tables():
        d = decay[...]
        a = jnp.exp(-d)
        mode_a[...] = a
        twice = 2.0 * d
        series = twice * (1.0 - twice * (0.5 - twice * (1.0 / 6 - twice * (1.0 / 24 - twice * (1.0 / 120)))))
        coef = residue[...] * jnp.sqrt(jnp.where(twice < 0.1, series, 1.0 - jnp.exp(-twice)))
        modal[...] = coef
        steps = lax.broadcasted_iota(jnp.int32, (CHUNKS, WIDTH), 0).astype(f32)
        for n in range(MODES):
            mode_b[n] = jnp.broadcast_to(mode_a[pl.ds(n, 1), :], (CHUNKS, WIDTH))
            mode_p[n] = jnp.exp(-decay[pl.ds(n, 1), :] * (steps * SPAN))
        lags = lax.broadcasted_iota(jnp.int32, (SPAN, WIDTH), 0).astype(f32)
        filt = jnp.zeros((SPAN, WIDTH), f32)
        for n in range(MODES):
            filt = filt + modal[pl.ds(n, 1), :] * jnp.exp(-decay[pl.ds(n, 1), :] * lags)
        filt = filt + jnp.where(lags == 0.0, skip[...], 0.0)
        for t in range(SPAN):
            mode_f[t] = jnp.broadcast_to(filt[t : t + 1, :], (CHUNKS, WIDTH))
        upad[pl.ds(0, SPAN)] = jnp.zeros((SPAN, CHUNKS, WIDTH), f32)
        there = far[c]
        fc, fsn = there[:, :HD], there[:, HD:]
        nc, ns = near[:, pl.ds(0, HD)], near[:, pl.ds(HD, HD)]
        cs[:, pl.ds(0, HD)] = nc * fc - ns * fsn
        lane = lax.broadcasted_iota(jnp.int32, (ROWS, HD), 1)
        sine = ns * fc + nc * fsn
        cs[:, pl.ds(HD, HD)] = jnp.where(lane < HD // 2, -sine, sine)

    def before_first():
        for copy in scopies[1:]:
            copy.wait()
        tables()
        sq[...] = jnp.zeros_like(sq)
        acc1[...] = jnp.zeros_like(acc1)
        for copy in wcopies[:3]:
            copy.wait()

    if STOP < 1:
        before_first()
    if STOP >= 1:
        gather(g1, 0, PARTS1, before_first, folder(g1, hgain, w1s, acc1), lambda n: None)

    if STOP >= 2:
        last = ROWS - 16
        halo_out[...] = (acc1[pl.ds(last, 16), :] * row_scale(last, 16)).astype(bf16)
        halo = pltpu.make_async_remote_copy(
            src_ref=halo_out, dst_ref=halo_in, send_sem=hsem.at[0], recv_sem=hsem.at[1],
            device_id={"ctx": lax.rem(c + 1, NC)}, device_id_type=MESH,
        )
        halo.start()
        for k in range(6):
            strm[k, pl.ds(0, 8), :] = jnp.zeros((8, 128), f32)

        def to_streams(i, _):
            lo = pl.multiple_of(i * 32, 32)
            block = (acc1[pl.ds(lo, 32), :] * row_scale(lo, 32)).astype(bf16)
            block = block.astype(f32)
            for k in range(6):
                strm[k, pl.ds(lo + 8, 32), :] = block[:, k * 128 : (k + 1) * 128]
            return 0

        lax.fori_loop(0, ROWS // 32, to_streams, 0)

        def tap(j, s):
            return taps[j, pl.ds(s, 1), :]

        def stream_rows(start):
            return jnp.concatenate(
                [strm[k, pl.ds(start, CHUNKS, stride=SPAN), :] for k in range(6)], axis=1
            )

        def short(now, one, two):
            out = []
            for s in range(3):
                cols = slice(s * WIDTH, (s + 1) * WIDTH)
                out.append(tap(0, s) * now[:, cols] + tap(1, s) * one[:, cols] + tap(2, s) * two[:, cols])
            return out

        def short_step(s, rows):
            one, two = rows
            now = stream_rows(s + 8)
            q, k, v = short(now, one, two)
            qs[s] = q
            upad[SPAN + s] = k * v
            return now, one

        lax.fori_loop(0, SPAN, short_step, (stream_rows(7), stream_rows(6)), unroll=UN)

    if STOP >= 3:
        def horner(s, state):
            u = upad[SPAN + s]
            return tuple(state[n] * mode_b[n] + u for n in range(MODES))

        zero = jnp.zeros((CHUNKS, WIDTH), f32)
        state = lax.fori_loop(0, SPAN, horner, (zero,) * MODES, unroll=UN)
        sub = lax.broadcasted_iota(jnp.int32, (CHUNKS, WIDTH), 0)
        for n in range(MODES):
            e = state[n]
            for k in (1, 2, 4):
                moved = jnp.where(sub >= k, pltpu.roll(e, k, 0), 0.0)
                e = e + mode_p[n, pl.ds(k, 1), :] * moved
            e_out[pl.ds(n, 1), :] = e[CHUNKS - 1 : CHUNKS, :]
            ends[n] = jnp.where(sub >= 1, pltpu.roll(e, 1, 0), 0.0)

        def inside(block):
            def lag(d, total):
                return total + mode_f[d][None] * upad[pl.ds(SPAN + block * 8 - d, 8)]

            conv[pl.ds(block * 8, 8)] = lax.fori_loop(
                0, block * 8 + 8, lag, jnp.zeros((8, CHUNKS, WIDTH), f32), unroll=UN
            )

        for block in range(3):
            inside(block)

        halo.wait_recv()
        before = jnp.where(c == 0, 0.0, halo_in[...].astype(f32)[14:16, :])
        first, second = [], []
        for s in range(3):
            two, one = (before[r : r + 1, s * WIDTH : (s + 1) * WIDTH] for r in range(2))
            now, then = (
                jnp.concatenate([strm[2 * s + k, pl.ds(8 + r, 1), :] for k in range(2)], axis=1)
                for r in range(2)
            )
            base = tap(0, s) * now
            first.append((base, tap(1, s) * one + tap(2, s) * two))
            base = tap(0, s) * then + tap(1, s) * now
            second.append((base, tap(2, s) * one))

        def product(pair):
            (k, dk), (v, dv) = pair[1:]
            return k * dv + dk * v + dk * dv

        du0, du1 = product(first), product(second)
        inverse = jnp.exp(decay[...])
        come = (du0 + du1 * inverse) * inverse
        whole = jnp.exp(-decay[...] * float(ROWS))
        e_out[...] += whole * come

        def state_copy(j):
            return pltpu.make_async_remote_copy(
                src_ref=e_out, dst_ref=e_in.at[chip], send_sem=es.at[j], recv_sem=er.at[chip],
                device_id={"ctx": 2 * j + core}, device_id_type=MESH,
            )

        for j in range(1, NC // 2):

            @pl.when(j > chip)
            def _():
                state_copy(j).start()

        inside(3)
        qs[0, pl.ds(0, 1), :] += first[0][1]
        qs[1, pl.ds(0, 1), :] += second[0][1]
        early = jnp.sum(modal[...] * inverse, axis=0, keepdims=True)
        conv[0, pl.ds(0, 1), :] += skip[...] * du0 - early * du1
        conv[1, pl.ds(0, 1), :] += skip[...] * du1
        double = whole * whole

        def arrive(i, total):
            pltpu.make_async_remote_copy(
                src_ref=e_out, dst_ref=e_in.at[i], send_sem=es.at[0], recv_sem=er.at[i],
                device_id={"ctx": c + sgn}, device_id_type=MESH,
            ).wait_recv()
            return total * double + e_in[i]

        same = lax.fori_loop(0, chip, arrive, jnp.zeros((MODES, WIDTH), f32))
        s_out[...] = jnp.where(core == 0, whole * (whole * same) + e_out[...], same)
        swap = pltpu.make_async_remote_copy(
            src_ref=s_out, dst_ref=s_in, send_sem=ssem.at[0], recv_sem=ssem.at[1],
            device_id={"ctx": c + sgn}, device_id_type=MESH,
        )
        swap.start()
        rise = modal[...] * mode_a[...]
        swap.wait_recv()
        inward = whole * same + s_in[...] + come
        begin = tuple(
            (ends[n] + inward[n : n + 1, :] * mode_p[n]) * rise[n : n + 1, :] for n in range(MODES)
        )

        def spread(t, state):
            total = conv[t]
            for n in range(MODES):
                total = total + state[n]
            gated = qs[t] * total
            for k in range(2):
                gate[k, pl.ds(t, CHUNKS, stride=SPAN), :] = gated[:, k * 128 : (k + 1) * 128]
            return tuple(state[n] * mode_b[n] for n in range(MODES))

        lax.fori_loop(0, SPAN, spread, begin, unroll=UN)
        for k in range(2):
            cols = pl.ds(k * 128, 128)
            g2[h, :, cols] = (g1[h, :, cols].astype(f32) + gate[k, pl.ds(0, ROWS), :]).astype(bf16)

    if STOP >= 4:
        out_copy = pltpu.make_async_copy(g2.at[h], mixed, osem)
        out_copy.start()

        def kv_copy(src, org, n, sem, to):
            return pltpu.make_async_remote_copy(
                src_ref=src, dst_ref=kvs.at[org, n], send_sem=sem, recv_sem=kr.at[org, n],
                device_id={"ctx": to}, device_id_type=MESH,
            )

        sibling = c + sgn

        half = NC // 4

        def kv_goes(j, n):
            if j < half or not TREE[n]:
                return j > chip
            return jnp.logical_or(j == chip + half, jnp.logical_and(j > chip, chip >= half))

        def relay_copy(j, n):
            org = c - 2 * half
            return kv_copy(kvs.at[org, n], org, n, rs.at[j - half, n], 2 * j + core)

        def relay(n):
            @pl.when(jnp.logical_and(chip >= half, TREE[n] == 1))
            def _():
                relay_copy(half, n).wait_recv()
                for j in range(half, 2 * half):

                    @pl.when(j != chip)
                    def _():
                        relay_copy(j, n).start()

        def finish(n):
            lo = n * GROUP
            here = pl.ds(lo, GROUP)
            rows = acc2[here, :] * row_scale(lo, GROUP)
            cosine, sine = cs[here, pl.ds(0, HD)], cs[here, pl.ds(HD, HD)]

            def turn(x):
                return x * cosine + pltpu.roll(x, HD // 2, 1) * sine

            kv[n, :, pl.ds(0, HD)] = turn(rows[:, HD : 2 * HD]).astype(bf16)
            kv[n, :, pl.ds(HD, HD)] = rows[:, 2 * HD :].T.astype(bf16)
            if STOP >= 5:
                for k in range(1, NC // 2):
                    j = NC // 2 - k if DESC else k

                    @pl.when(kv_goes(j, n))
                    def _(j=j):
                        kv_copy(kv.at[n], c, n, ks.at[j, n], 2 * j + core).start()

                @pl.when(core == 0)
                def _():
                    kv_copy(kv.at[n], c, n, ks.at[0, n], sibling).start()

            qt[:, here] = turn(rows[:, :HD]).T.astype(bf16)

        def before_second():
            sq[...] = jnp.zeros_like(sq)
            acc2[...] = jnp.zeros_like(acc2)
            for copy in wcopies[3:]:
                copy.wait()

        def finished(n):
            if len(PARTS2) > 1:
                finish(n)
            else:
                finish(0)
                finish(1)

            if STOP >= 5 and n == 1:
                relay(0)

        gather(g2, 1, PARTS2, before_second, folder(g2, again, w2s, acc2), finished)

    def settle():
        if STOP >= 1:
            sent(g1, 0, PARTS1)
        if STOP >= 2:
            halo.wait_send()
        if STOP == 2:
            halo.wait_recv()
        if STOP >= 3:
            swap.wait_send()
            for j in range(1, NC // 2):

                @pl.when(j > chip)
                def _():
                    state_copy(j).wait_send()

        if STOP >= 4:
            sent(g2, 1, PARTS2)
            out_copy.wait()
        if STOP >= 5:
            for n in range(2):

                @pl.when(core == 0)
                def _():
                    kv_copy(kv.at[n], c, n, ks.at[0, n], sibling).wait_send()

                for j in range(1, NC // 2):

                    @pl.when(kv_goes(j, n))
                    def _():
                        kv_copy(kv.at[n], c, n, ks.at[j, n], 2 * j + core).wait_send()

    if STOP >= 5:
        factor = 1.0 / HD**0.5

        def attend(refs, diagonal):
            keys = jnp.concatenate([ref[:, pl.ds(0, HD)] for ref in refs], axis=0)
            scores = jnp.dot(keys, qt[...], preferred_element_type=f32) * factor
            if diagonal:
                key = lax.broadcasted_iota(jnp.int32, scores.shape, 0)
                query = lax.broadcasted_iota(jnp.int32, scores.shape, 1)
                scores = jnp.where(key <= query, scores, -1e30)
            best = jnp.max(scores, axis=0, keepdims=True)
            if not diagonal:
                best = jnp.maximum(best, m_s[...])
            weights = jnp.exp(scores - best)
            sums = jnp.sum(weights, axis=0, keepdims=True)
            values = jnp.concatenate([ref[:, pl.ds(HD, HD)] for ref in refs], axis=1)
            update = jnp.dot(values, weights.astype(bf16), preferred_element_type=f32)
            if diagonal:
                l_s[...] = sums
                o_s[...] = update
            else:
                rescale = jnp.exp(m_s[...] - best)
                l_s[...] = l_s[...] * rescale + sums
                o_s[...] = o_s[...] * rescale + update
            m_s[...] = best

        def origin(k):
            return 2 * (chip - 1 - k) + core

        def pass_on(k, n):
            org = origin(k)

            @pl.when(jnp.logical_or(org != c - 2 * half, TREE[n] == 0))
            def _():
                kv_copy(kv.at[n], org, n, ks.at[0, n], sibling).wait_recv()

            kv_copy(kvs.at[org, n], org, n, fs.at[k, n], sibling).start()

        def both_cores(k, n):
            org = origin(k)
            other = org + sgn
            kv_copy(kv.at[n], other, n, ks.at[0, n], sibling).wait_recv()
            if not NOATT:
                attend((kvs.at[org, n], kvs.at[other, n]), False)

        attend((kv.at[0], kv.at[1]), True)

        def pass_first(k, _):
            pass_on(k, 0)
            return 0

        lax.fori_loop(0, chip, pass_first, 0)
        relay(1)

        @pl.when(core == 1)
        def _():
            for n in range(2):
                kv_copy(kv.at[n], c - 1, n, ks.at[0, n], 0).wait_recv()
            attend((kvs.at[c - 1, 0], kvs.at[c - 1, 1]), False)

        def attend_first(k, _):
            both_cores(k, 0)
            return 0

        lax.fori_loop(0, chip, attend_first, 0)
        settle()

        def lagged(k, _):
            @pl.when(k < chip)
            def _():
                pass_on(k, 1)

            @pl.when(k >= LAG1)
            def _():
                both_cores(k - LAG1, 1)

            return 0

        lax.fori_loop(0, jnp.where(chip > 0, chip + LAG1, 0), lagged, 0)

        att[...] = (o_s[...] / l_s[...]).T.astype(bf16)
        att_copy = pltpu.make_async_copy(att, attended, asem)
        att_copy.start()

    if STOP < 5:
        if STOP < 4:
            for copy in wcopies[3:]:
                copy.wait()
        settle()
    if STOP >= 5:
        for n in range(2):
            for j in range(half, 2 * half):

                @pl.when(jnp.logical_and(chip >= half, j != chip) if TREE[n] else False)
                def _():
                    relay_copy(j, n).wait_send()

            def passed(k, _):
                org = origin(k)
                kv_copy(kvs.at[org, n], org, n, fs.at[k, n], sibling).wait_send()
                return 0

            lax.fori_loop(0, chip, passed, 0)
        att_copy.wait()


def write(mixed_in, attended_in, mixed, attended, one, two, sem):
    loads = (
        pltpu.make_async_copy(mixed_in, one, sem.at[0]),
        pltpu.make_async_copy(attended_in, two, sem.at[1]),
    )
    stores = (
        pltpu.make_async_copy(one, mixed, sem.at[2]),
        pltpu.make_async_copy(two, attended, sem.at[3]),
    )
    for copy in loads:
        copy.start()
    for load, store in zip(loads, stores):
        load.wait()
        store.start()
    for copy in stores:
        copy.wait()


def local(residual, hyena_gain, in_weight, short_filter, decay_rate, residue, skip_gain, attn_gain, qkv_weight):
    far, near = rope_tables()
    vmem = pl.BlockSpec(memory_space=pltpu.VMEM)
    hbm = pl.BlockSpec(memory_space=pltpu.MemorySpace.HBM)
    dma = pltpu.SemaphoreType.DMA
    done = pl.pallas_call(
        kernel,
        out_shape=(
            jax.ShapeDtypeStruct((ROWS, WIDTH), bf16),
            jax.ShapeDtypeStruct((ROWS, HD), bf16),
        ),
        in_specs=[hbm] * 11,
        out_specs=(hbm, hbm),
        scratch_shapes=[
            pltpu.VMEM((1, NH * WIDTH), f32),
            pltpu.VMEM((3, 3, WIDTH), f32),
            pltpu.VMEM((MODES, WIDTH), f32),
            pltpu.VMEM((MODES, WIDTH), f32),
            pltpu.VMEM((1, WIDTH), f32),
            pltpu.VMEM((1, NH * WIDTH), f32),
            pltpu.VMEM((NC, 1, 2 * HD), f32),
            pltpu.VMEM((ROWS, 2 * HD), f32),
            pltpu.VMEM((NH, ROWS, WIDTH), bf16),
            pltpu.VMEM((NH, ROWS, WIDTH), bf16),
            pltpu.VMEM((NH * WIDTH, 3 * WIDTH), bf16),
            pltpu.VMEM((NH * WIDTH, 3 * HD), bf16),
            pltpu.VMEM((ROWS, 3 * WIDTH), f32),
            pltpu.VMEM((ROWS, 3 * HD), f32),
            pltpu.VMEM((ROWS, 128), f32),
            pltpu.VMEM((6, ROWS + 8 + SPAN, 128), f32),
            pltpu.VMEM((16, 3 * WIDTH), bf16),
            pltpu.VMEM((16, 3 * WIDTH), bf16),
            pltpu.VMEM((MODES, WIDTH), f32),
            pltpu.VMEM((MODES, CHUNKS, WIDTH), f32),
            pltpu.VMEM((MODES, CHUNKS, WIDTH), f32),
            pltpu.VMEM((SPAN, CHUNKS, WIDTH), f32),
            pltpu.VMEM((MODES, WIDTH), f32),
            pltpu.VMEM((2 * SPAN, CHUNKS, WIDTH), f32),
            pltpu.VMEM((SPAN, CHUNKS, WIDTH), f32),
            pltpu.VMEM((SPAN, CHUNKS, WIDTH), f32),
            pltpu.VMEM((MODES, CHUNKS, WIDTH), f32),
            pltpu.VMEM((2, ROWS + SPAN, 128), f32),
            pltpu.VMEM((MODES, WIDTH), f32),
            pltpu.VMEM((NC // 2, MODES, WIDTH), f32),
            pltpu.VMEM((MODES, WIDTH), f32),
            pltpu.VMEM((MODES, WIDTH), f32),
            pltpu.VMEM((ROWS, 2 * HD), f32),
            pltpu.VMEM((HD, ROWS), bf16),
            pltpu.VMEM((2, GROUP, 2 * HD), bf16),
            pltpu.VMEM((NC, 2, GROUP, 2 * HD), bf16),
            pltpu.VMEM((1, ROWS), f32),
            pltpu.VMEM((1, ROWS), f32),
            pltpu.VMEM((HD, ROWS), f32),
            pltpu.VMEM((ROWS, HD), bf16),
            dma((9,)),
            dma,
            dma,
            dma((6,)),
            dma((2, 8)),
            dma((2, 8, NH)),
            dma((2,)),
            dma((2,)),
            dma((NC,)),
            dma((NC,)),
            dma((NC // 2, 2)),
            dma((NC, 2)),
            dma((NC // 2, 2)),
            dma((NC // 4, 2)),
        ],
        compiler_params=pltpu.CompilerParams(
            collective_id=1, has_side_effects=True, vmem_limit_bytes=56 << 20
        ),
        name="genome",
    )(
        residual,
        hyena_gain.reshape(1, -1),
        in_weight.transpose(1, 0, 2),
        short_filter,
        decay_rate.T,
        residue.T,
        skip_gain.reshape(1, -1),
        attn_gain.reshape(1, -1),
        qkv_weight.transpose(1, 0, 2),
        far.reshape(NC, 1, -1),
        near,
    )
    return pl.pallas_call(
        write,
        out_shape=(
            jax.ShapeDtypeStruct((ROWS, WIDTH), bf16),
            jax.ShapeDtypeStruct((ROWS, HD), bf16),
        ),
        in_specs=[hbm, hbm],
        out_specs=(hbm, hbm),
        scratch_shapes=[
            pltpu.VMEM((ROWS, WIDTH), bf16),
            pltpu.VMEM((ROWS, HD), bf16),
            dma((4,)),
        ],
        compiler_params=pltpu.CompilerParams(vmem_limit_bytes=56 << 20),
        name="write",
    )(*done)


def solution(mesh):
    return jax.shard_map(
        local,
        mesh=mesh,
        in_specs=(
            P("ctx", "head"),
            P(),
            P(None, None, "head"),
            P(None, None, "head"),
            P("head", None),
            P("head", None),
            P("head"),
            P(),
            P(None, None, "head"),
        ),
        out_specs=(P("ctx", "head"), P("ctx", "head")),
        check_vma=False,
    )
```

```python
import functools

import jax
import jax.numpy as jnp
import numpy as np
from jax import lax
from jax.experimental import pallas as pl
from jax.experimental.pallas import tpu as pltpu
from jax.sharding import PartitionSpec as P

MESH = pl.DeviceIdType.MESH
f32 = jnp.float32
bf16 = jnp.bfloat16

HD = 128
EPS = 1e-6
ROWS = 256
WIDTH = 256
NH = 16
NC = 16
NZ = 8
MODES = 16
SPAN = 32
CHUNKS = 8
STOP = 9
NOATT = 0
TREE = (0, 1)
DESC = 1
UN = 4
LAG0 = 8
LAG1 = 6
NOFOLD = 0
DIST = 4
PARTS1 = (((0, 64, 0), (64, 32, 1), (96, 64, 0), (160, 32, 1), (192, 32, 0), (224, 32, 1)),)
PARTS2 = (((0, 80, 0), (80, 48, 1)), ((128, 80, 0), (208, 48, 1)))
GROUP = 128
KVORDER = 1


def rope_tables():
    half = HD // 2
    inverse = 10000.0 ** (-np.arange(half) / half)

    def table(positions):
        angle = positions[:, None] * inverse[None, :]
        cos, sin = np.cos(angle), np.sin(angle)
        return np.concatenate([cos, cos, sin, sin], axis=1).astype(np.float32)

    return table(np.arange(NC) * float(ROWS)), table(np.arange(ROWS) * 1.0)


def kernel(
    res_h, hgain_h, w1, taps_h, decay_h, residue_h, skip_h, again_h, w2, far_h, near_h,
    mixed, attended,
    hgain, taps, decay, residue, skip, again, far, near,
    g1, g2, w1s, w2s, acc1, acc2, sq, strm, halo_out, halo_in,
    mode_a, mode_b, mode_p, mode_f, modal, upad, qs, conv, ends, gate, e_out, e_in, s_out, s_in,
    cs, qt, kv, kvs, m_s, l_s, o_s, att,
    psem, osem, asem, wsem, gs, gr, hsem, ssem, es, er, ks, kr, fs, rs,
):
    c = lax.axis_index("ctx")
    h = lax.axis_index("head")
    core = lax.rem(c, 2)
    sgn = 1 - 2 * core
    z = lax.rem(h, NZ)
    xh = h // NZ
    chip = c // 2

    def head(x, zz):
        return x * NZ + lax.rem(zz + 2 * NZ, NZ)

    partner = head(1 - xh, z)
    ahead = head(xh, z + sgn)
    behind = head(xh, z - sgn)

    small = ((res_h, g1.at[h]), (decay_h, decay), (residue_h, residue), (skip_h, skip), (hgain_h, hgain),
             (taps_h, taps), (far_h, far), (near_h, near), (again_h, again))
    scopies = [pltpu.make_async_copy(a, b, psem.at[k]) for k, (a, b) in enumerate(small)]
    for copy in scopies:
        copy.start()
    wcopies = []
    for j in range(3):
        wcopies.append(pltpu.make_async_copy(w1.at[j], w1s.at[:, pl.ds(j * WIDTH, WIDTH)], wsem.at[j]))
    for j in range(3):
        wcopies.append(pltpu.make_async_copy(w2.at[j], w2s.at[:, pl.ds(j * HD, HD)], wsem.at[3 + j]))
    for copy in wcopies:
        copy.start()

    barrier = pltpu.get_barrier_semaphore()
    slant, slant_back = head(1 - xh, z + sgn), head(1 - xh, z - sgn)
    for to in (partner, ahead, behind, slant, slant_back):
        pl.semaphore_signal(barrier, inc=1, device_id={"head": to}, device_id_type=MESH)
    for k in range(1, NC // 2):
        to = 2 * lax.rem(chip + k, NC // 2) + core
        pl.semaphore_signal(barrier, inc=1, device_id={"ctx": to}, device_id_type=MESH)
    for k in (1, NC - 1):
        pl.semaphore_signal(
            barrier, inc=1, device_id={"ctx": lax.rem(c + k, NC)}, device_id_type=MESH
        )
    pl.semaphore_wait(barrier, 5 + NC // 2 - 1 + 2)
    scopies[0].wait()


    def gather(g, which, groups, prepare, fold, done):
        numbers, count = [], 0
        for group in groups:
            numbers.append(range(count, count + len(group)))
            count += len(group)
        flat = [part for group in groups for part in group]

        def copy(p, org, to):
            rows = g.at[org, pl.ds(flat[p][0], flat[p][1])]
            return pltpu.make_async_remote_copy(
                src_ref=rows, dst_ref=rows, send_sem=gs.at[which, p], recv_sem=gr.at[which, p, org],
                device_id={"head": to}, device_id_type=MESH,
            )

        def send(p, org, to):
            copy(p, org, to).start()

        def wait(p, org):
            copy(p, org, partner).wait_recv()

        def begin(n):
            for p in numbers[n]:
                if flat[p][2]:
                    send(p, h, slant)
                    send(p, h, slant_back)
            for p in numbers[n]:
                send(p, h, ahead)
                send(p, h, behind)
            for p in numbers[n]:
                send(p, h, partner)

        def step(n, d, between=lambda j: None):
            a, b = head(xh, z - sgn * d), head(xh, z + sgn * d)
            a2, b2 = head(1 - xh, z - sgn * d), head(1 - xh, z + sgn * d)

            def hop(p, org, to, far, over):
                wait(p, org)

                @pl.when(d < far)
                def _():
                    send(p, org, to)
                    if over and far == 3:
                        send(p, org, partner)

                if over and far == 3:

                    @pl.when(d == 3)
                    def _():
                        send(p, org, partner)

                if over and far == 4:

                    @pl.when(d == 3)
                    def _():
                        send(p, org, slant)

                    @pl.when(d < 4)
                    def _():
                        send(p, org, partner)

            def both(p, first, second, to, back, over):
                hop(p, first, to, 4, over)

                @pl.when(d < 4)
                def _():
                    hop(p, second, back, 3, over)

            calls = [(p, a, b, ahead, behind, not flat[p][2]) for p in numbers[n]]
            calls += [(p, b2, a2, behind, ahead, False) for p in numbers[n] if flat[p][2]]
            for i, call in enumerate(calls):
                both(*call)
                for j in range(4 * i // len(calls), 4 * (i + 1) // len(calls)):
                    between(j)

        def folds(n, d):
            def one(j):
                over = j >= jnp.where(d == 1, 3, jnp.where(d == 4, 1, 2))
                here = jnp.where(d == 1, j, 2 * d - 1 + j)
                there = jnp.where(d == 1, 0, jnp.where(d == 4, 4 + j, 2 * d - 5 + j))
                k = jnp.where(over, there, here)
                apart = jnp.where(k % 2 == 1, -((k + 1) // 2), k // 2)
                org = head(jnp.where(over, 1 - xh, xh), z + sgn * apart)

                @pl.when(over)
                def _():
                    for p in numbers[n]:
                        if not flat[p][2]:
                            wait(p, org)

                @pl.when(jnp.logical_and(over, k == 0))
                def _():
                    for p in numbers[n]:
                        if flat[p][2]:
                            wait(p, org)

                if not NOFOLD:
                    fold(groups[n], org)

            return one

        def some_folds(n, d, lo, hi):
            one = folds(n, d)

            def body(j, _):
                one(j)
                return 0

            lax.fori_loop(lo, hi, body, 0)

        def final(n):
            a, b2 = head(xh, z + 4), head(1 - xh, z + 4)
            for p in numbers[n]:
                wait(p, a)
            some_folds(n, 3, 0, 4)
            some_folds(n, 4, 0, 3)
            for p in numbers[n]:
                if flat[p][2]:
                    wait(p, b2)
            some_folds(n, 4, 3, 4)
            done(n)

        lag = len(groups) > 1
        for n in range(len(groups)):
            begin(n)
        step(0, 1)
        prepare()

        def later(d, _):
            step(0, d, folds(0, d - 1))
            if lag:
                step(1, d - 1)

                @pl.when(d > 2)
                def _():
                    some_folds(1, d - 2, 0, 4)

            return 0

        lax.fori_loop(2, 4, later, 0)
        if lag:
            step(1, 3)
        final(0)
        if lag:
            some_folds(1, 2, 0, 4)
            final(1)

    def sent(g, which, groups):
        for p, part in enumerate(part for group in groups for part in group):
            rows = g.at[pl.ds(0, NH - 1), pl.ds(part[0], part[1])]
            pltpu.make_async_remote_copy(
                src_ref=rows, dst_ref=rows, send_sem=gs.at[which, p], recv_sem=gr.at[which, p, 0],
                device_id={"head": partner}, device_id_type=MESH,
            ).wait_send()

    def folder(g, gain, w, acc):
        def fold(group, org):
            lo, n = group[0][0], sum(part[1] for part in group)
            here = pl.ds(lo, n)
            columns = pl.ds(pl.multiple_of(org * WIDTH, WIDTH), WIDTH)
            rows = g[org, here].astype(f32)
            squares = rows * rows
            sq[here, :] += squares[:, :128] + squares[:, 128:]
            scaled = (rows * gain[:, columns]).astype(bf16)
            acc[here, :] += jnp.dot(scaled, w[columns, :], preferred_element_type=f32)

        return fold

    def row_scale(lo, n):
        total = jnp.sum(sq[pl.ds(lo, n), :], axis=1, keepdims=True)
        return lax.rsqrt(total * (1.0 / (NH * WIDTH)) + EPS)

    def tables():
        d = decay[...]
        a = jnp.exp(-d)
        mode_a[...] = a
        twice = 2.0 * d
        series = twice * (1.0 - twice * (0.5 - twice * (1.0 / 6 - twice * (1.0 / 24 - twice * (1.0 / 120)))))
        coef = residue[...] * jnp.sqrt(jnp.where(twice < 0.1, series, 1.0 - jnp.exp(-twice)))
        modal[...] = coef
        steps = lax.broadcasted_iota(jnp.int32, (CHUNKS, WIDTH), 0).astype(f32)
        for n in range(MODES):
            mode_b[n] = jnp.broadcast_to(mode_a[pl.ds(n, 1), :], (CHUNKS, WIDTH))
            mode_p[n] = jnp.exp(-decay[pl.ds(n, 1), :] * (steps * SPAN))
        lags = lax.broadcasted_iota(jnp.int32, (SPAN, WIDTH), 0).astype(f32)
        filt = jnp.zeros((SPAN, WIDTH), f32)
        for n in range(MODES):
            filt = filt + modal[pl.ds(n, 1), :] * jnp.exp(-decay[pl.ds(n, 1), :] * lags)
        filt = filt + jnp.where(lags == 0.0, skip[...], 0.0)
        for t in range(SPAN):
            mode_f[t] = jnp.broadcast_to(filt[t : t + 1, :], (CHUNKS, WIDTH))
        upad[pl.ds(0, SPAN)] = jnp.zeros((SPAN, CHUNKS, WIDTH), f32)
        there = far[c]
        fc, fsn = there[:, :HD], there[:, HD:]
        nc, ns = near[:, pl.ds(0, HD)], near[:, pl.ds(HD, HD)]
        cs[:, pl.ds(0, HD)] = nc * fc - ns * fsn
        lane = lax.broadcasted_iota(jnp.int32, (ROWS, HD), 1)
        sine = ns * fc + nc * fsn
        cs[:, pl.ds(HD, HD)] = jnp.where(lane < HD // 2, -sine, sine)

    def before_first():
        for copy in scopies[1:]:
            copy.wait()
        tables()
        sq[...] = jnp.zeros_like(sq)
        acc1[...] = jnp.zeros_like(acc1)
        for copy in wcopies[:3]:
            copy.wait()

    if STOP < 1:
        before_first()
    if STOP >= 1:
        gather(g1, 0, PARTS1, before_first, folder(g1, hgain, w1s, acc1), lambda n: None)

    if STOP >= 2:
        last = ROWS - 16
        halo_out[...] = (acc1[pl.ds(last, 16), :] * row_scale(last, 16)).astype(bf16)
        halo = pltpu.make_async_remote_copy(
            src_ref=halo_out, dst_ref=halo_in, send_sem=hsem.at[0], recv_sem=hsem.at[1],
            device_id={"ctx": lax.rem(c + 1, NC)}, device_id_type=MESH,
        )
        halo.start()
        for k in range(6):
            strm[k, pl.ds(0, 8), :] = jnp.zeros((8, 128), f32)

        def to_streams(i, _):
            lo = pl.multiple_of(i * 32, 32)
            block = (acc1[pl.ds(lo, 32), :] * row_scale(lo, 32)).astype(bf16)
            block = block.astype(f32)
            for k in range(6):
                strm[k, pl.ds(lo + 8, 32), :] = block[:, k * 128 : (k + 1) * 128]
            return 0

        lax.fori_loop(0, ROWS // 32, to_streams, 0)

        def tap(j, s):
            return taps[j, pl.ds(s, 1), :]

        def stream_rows(start):
            return jnp.concatenate(
                [strm[k, pl.ds(start, CHUNKS, stride=SPAN), :] for k in range(6)], axis=1
            )

        def short(now, one, two):
            out = []
            for s in range(3):
                cols = slice(s * WIDTH, (s + 1) * WIDTH)
                out.append(tap(0, s) * now[:, cols] + tap(1, s) * one[:, cols] + tap(2, s) * two[:, cols])
            return out

        def short_step(s, rows):
            one, two = rows
            now = stream_rows(s + 8)
            q, k, v = short(now, one, two)
            qs[s] = q
            upad[SPAN + s] = k * v
            return now, one

        lax.fori_loop(0, SPAN, short_step, (stream_rows(7), stream_rows(6)), unroll=UN)

    if STOP >= 3:
        def horner(s, state):
            u = upad[SPAN + s]
            return tuple(state[n] * mode_b[n] + u for n in range(MODES))

        zero = jnp.zeros((CHUNKS, WIDTH), f32)
        state = lax.fori_loop(0, SPAN, horner, (zero,) * MODES, unroll=UN)
        sub = lax.broadcasted_iota(jnp.int32, (CHUNKS, WIDTH), 0)
        for n in range(MODES):
            e = state[n]
            for k in (1, 2, 4):
                moved = jnp.where(sub >= k, pltpu.roll(e, k, 0), 0.0)
                e = e + mode_p[n, pl.ds(k, 1), :] * moved
            e_out[pl.ds(n, 1), :] = e[CHUNKS - 1 : CHUNKS, :]
            ends[n] = jnp.where(sub >= 1, pltpu.roll(e, 1, 0), 0.0)

        def inside(block):
            def lag(d, total):
                return total + mode_f[d][None] * upad[pl.ds(SPAN + block * 8 - d, 8)]

            conv[pl.ds(block * 8, 8)] = lax.fori_loop(
                0, block * 8 + 8, lag, jnp.zeros((8, CHUNKS, WIDTH), f32), unroll=UN
            )

        for block in range(3):
            inside(block)

        halo.wait_recv()
        before = jnp.where(c == 0, 0.0, halo_in[...].astype(f32)[14:16, :])
        first, second = [], []
        for s in range(3):
            two, one = (before[r : r + 1, s * WIDTH : (s + 1) * WIDTH] for r in range(2))
            now, then = (
                jnp.concatenate([strm[2 * s + k, pl.ds(8 + r, 1), :] for k in range(2)], axis=1)
                for r in range(2)
            )
            base = tap(0, s) * now
            first.append((base, tap(1, s) * one + tap(2, s) * two))
            base = tap(0, s) * then + tap(1, s) * now
            second.append((base, tap(2, s) * one))

        def product(pair):
            (k, dk), (v, dv) = pair[1:]
            return k * dv + dk * v + dk * dv

        du0, du1 = product(first), product(second)
        inverse = jnp.exp(decay[...])
        come = (du0 + du1 * inverse) * inverse
        whole = jnp.exp(-decay[...] * float(ROWS))
        e_out[...] += whole * come

        def state_copy(j):
            return pltpu.make_async_remote_copy(
                src_ref=e_out, dst_ref=e_in.at[chip], send_sem=es.at[j], recv_sem=er.at[chip],
                device_id={"ctx": 2 * j + core}, device_id_type=MESH,
            )

        for j in range(1, NC // 2):

            @pl.when(j > chip)
            def _():
                state_copy(j).start()

        inside(3)
        qs[0, pl.ds(0, 1), :] += first[0][1]
        qs[1, pl.ds(0, 1), :] += second[0][1]
        early = jnp.sum(modal[...] * inverse, axis=0, keepdims=True)
        conv[0, pl.ds(0, 1), :] += skip[...] * du0 - early * du1
        conv[1, pl.ds(0, 1), :] += skip[...] * du1
        double = whole * whole

        def arrive(i, total):
            pltpu.make_async_remote_copy(
                src_ref=e_out, dst_ref=e_in.at[i], send_sem=es.at[0], recv_sem=er.at[i],
                device_id={"ctx": c + sgn}, device_id_type=MESH,
            ).wait_recv()
            return total * double + e_in[i]

        same = lax.fori_loop(0, chip, arrive, jnp.zeros((MODES, WIDTH), f32))
        s_out[...] = jnp.where(core == 0, whole * (whole * same) + e_out[...], same)
        swap = pltpu.make_async_remote_copy(
            src_ref=s_out, dst_ref=s_in, send_sem=ssem.at[0], recv_sem=ssem.at[1],
            device_id={"ctx": c + sgn}, device_id_type=MESH,
        )
        swap.start()
        rise = modal[...] * mode_a[...]
        swap.wait_recv()
        inward = whole * same + s_in[...] + come
        begin = tuple(
            (ends[n] + inward[n : n + 1, :] * mode_p[n]) * rise[n : n + 1, :] for n in range(MODES)
        )

        def spread(t, state):
            total = conv[t]
            for n in range(MODES):
                total = total + state[n]
            gated = qs[t] * total
            for k in range(2):
                gate[k, pl.ds(t, CHUNKS, stride=SPAN), :] = gated[:, k * 128 : (k + 1) * 128]
            return tuple(state[n] * mode_b[n] for n in range(MODES))

        lax.fori_loop(0, SPAN, spread, begin, unroll=UN)
        for k in range(2):
            cols = pl.ds(k * 128, 128)
            g2[h, :, cols] = (g1[h, :, cols].astype(f32) + gate[k, pl.ds(0, ROWS), :]).astype(bf16)

    if STOP >= 4:
        out_copy = pltpu.make_async_copy(g2.at[h], mixed, osem)
        out_copy.start()

        def kv_copy(src, org, n, sem, to):
            return pltpu.make_async_remote_copy(
                src_ref=src, dst_ref=kvs.at[org, n], send_sem=sem, recv_sem=kr.at[org, n],
                device_id={"ctx": to}, device_id_type=MESH,
            )

        sibling = c + sgn

        half = NC // 4

        def kv_goes(j, n):
            if j < half or not TREE[n]:
                return j > chip
            return jnp.logical_or(j == chip + half, jnp.logical_and(j > chip, chip >= half))

        def relay_copy(j, n):
            org = c - 2 * half
            return kv_copy(kvs.at[org, n], org, n, rs.at[j - half, n], 2 * j + core)

        def relay(n):
            @pl.when(jnp.logical_and(chip >= half, TREE[n] == 1))
            def _():
                relay_copy(half, n).wait_recv()
                for j in range(half, 2 * half):

                    @pl.when(j != chip)
                    def _():
                        relay_copy(j, n).start()

        def finish(n):
            lo = n * GROUP
            here = pl.ds(lo, GROUP)
            rows = acc2[here, :] * row_scale(lo, GROUP)
            cosine, sine = cs[here, pl.ds(0, HD)], cs[here, pl.ds(HD, HD)]

            def turn(x):
                return x * cosine + pltpu.roll(x, HD // 2, 1) * sine

            kv[n, :, pl.ds(0, HD)] = turn(rows[:, HD : 2 * HD]).astype(bf16)
            kv[n, :, pl.ds(HD, HD)] = rows[:, 2 * HD :].T.astype(bf16)
            if STOP >= 5:
                for k in range(1, NC // 2):
                    j = NC // 2 - k if DESC else k

                    @pl.when(kv_goes(j, n))
                    def _(j=j):
                        kv_copy(kv.at[n], c, n, ks.at[j, n], 2 * j + core).start()

                @pl.when(core == 0)
                def _():
                    kv_copy(kv.at[n], c, n, ks.at[0, n], sibling).start()

            qt[:, here] = turn(rows[:, :HD]).T.astype(bf16)

        def before_second():
            sq[...] = jnp.zeros_like(sq)
            acc2[...] = jnp.zeros_like(acc2)
            for copy in wcopies[3:]:
                copy.wait()

        def finished(n):
            if len(PARTS2) > 1:
                finish(n)
            else:
                finish(0)
                finish(1)

            if STOP >= 5 and n == 1:
                relay(0)

        gather(g2, 1, PARTS2, before_second, folder(g2, again, w2s, acc2), finished)

    def settle():
        if STOP >= 1:
            sent(g1, 0, PARTS1)
        if STOP >= 2:
            halo.wait_send()
        if STOP == 2:
            halo.wait_recv()
        if STOP >= 3:
            swap.wait_send()
            for j in range(1, NC // 2):

                @pl.when(j > chip)
                def _():
                    state_copy(j).wait_send()

        if STOP >= 4:
            sent(g2, 1, PARTS2)
            out_copy.wait()
        if STOP >= 5:
            for n in range(2):

                @pl.when(core == 0)
                def _():
                    kv_copy(kv.at[n], c, n, ks.at[0, n], sibling).wait_send()

                for j in range(1, NC // 2):

                    @pl.when(kv_goes(j, n))
                    def _():
                        kv_copy(kv.at[n], c, n, ks.at[j, n], 2 * j + core).wait_send()

    if STOP >= 5:
        factor = 1.0 / HD**0.5

        def attend(refs, diagonal):
            keys = jnp.concatenate([ref[:, pl.ds(0, HD)] for ref in refs], axis=0)
            scores = jnp.dot(keys, qt[...], preferred_element_type=f32) * factor
            if diagonal:
                key = lax.broadcasted_iota(jnp.int32, scores.shape, 0)
                query = lax.broadcasted_iota(jnp.int32, scores.shape, 1)
                scores = jnp.where(key <= query, scores, -1e30)
            best = jnp.max(scores, axis=0, keepdims=True)
            if not diagonal:
                best = jnp.maximum(best, m_s[...])
            weights = jnp.exp(scores - best)
            sums = jnp.sum(weights, axis=0, keepdims=True)
            values = jnp.concatenate([ref[:, pl.ds(HD, HD)] for ref in refs], axis=1)
            update = jnp.dot(values, weights.astype(bf16), preferred_element_type=f32)
            if diagonal:
                l_s[...] = sums
                o_s[...] = update
            else:
                rescale = jnp.exp(m_s[...] - best)
                l_s[...] = l_s[...] * rescale + sums
                o_s[...] = o_s[...] * rescale + update
            m_s[...] = best

        def origin(k):
            return 2 * (chip - 1 - k) + core

        def pass_on(k, n):
            org = origin(k)

            @pl.when(jnp.logical_or(org != c - 2 * half, TREE[n] == 0))
            def _():
                kv_copy(kv.at[n], org, n, ks.at[0, n], sibling).wait_recv()

            kv_copy(kvs.at[org, n], org, n, fs.at[k, n], sibling).start()

        def both_cores(k, n):
            org = origin(k)
            other = org + sgn
            kv_copy(kv.at[n], other, n, ks.at[0, n], sibling).wait_recv()
            if not NOATT:
                attend((kvs.at[org, n], kvs.at[other, n]), False)

        attend((kv.at[0], kv.at[1]), True)

        def pass_first(k, _):
            pass_on(k, 0)
            return 0

        lax.fori_loop(0, chip, pass_first, 0)
        relay(1)

        @pl.when(core == 1)
        def _():
            for n in range(2):
                kv_copy(kv.at[n], c - 1, n, ks.at[0, n], 0).wait_recv()
            attend((kvs.at[c - 1, 0], kvs.at[c - 1, 1]), False)

        def attend_first(k, _):
            both_cores(k, 0)
            return 0

        lax.fori_loop(0, chip, attend_first, 0)
        settle()

        def lagged(k, _):
            @pl.when(k < chip)
            def _():
                pass_on(k, 1)

            @pl.when(k >= LAG1)
            def _():
                both_cores(k - LAG1, 1)

            return 0

        lax.fori_loop(0, jnp.where(chip > 0, chip + LAG1, 0), lagged, 0)

        att[...] = (o_s[...] / l_s[...]).T.astype(bf16)
        att_copy = pltpu.make_async_copy(att, attended, asem)
        att_copy.start()

    if STOP < 5:
        if STOP < 4:
            for copy in wcopies[3:]:
                copy.wait()
        settle()
    if STOP >= 5:
        for n in range(2):
            for j in range(half, 2 * half):

                @pl.when(jnp.logical_and(chip >= half, j != chip) if TREE[n] else False)
                def _():
                    relay_copy(j, n).wait_send()

            def passed(k, _):
                org = origin(k)
                kv_copy(kvs.at[org, n], org, n, fs.at[k, n], sibling).wait_send()
                return 0

            lax.fori_loop(0, chip, passed, 0)
        att_copy.wait()


def write(mixed_in, attended_in, mixed, attended, one, two, sem):
    loads = (
        pltpu.make_async_copy(mixed_in, one, sem.at[0]),
        pltpu.make_async_copy(attended_in, two, sem.at[1]),
    )
    stores = (
        pltpu.make_async_copy(one, mixed, sem.at[2]),
        pltpu.make_async_copy(two, attended, sem.at[3]),
    )
    for copy in loads:
        copy.start()
    for load, store in zip(loads, stores):
        load.wait()
        store.start()
    for copy in stores:
        copy.wait()


def local(residual, hyena_gain, in_weight, short_filter, decay_rate, residue, skip_gain, attn_gain, qkv_weight):
    far, near = rope_tables()
    vmem = pl.BlockSpec(memory_space=pltpu.VMEM)
    hbm = pl.BlockSpec(memory_space=pltpu.MemorySpace.HBM)
    dma = pltpu.SemaphoreType.DMA
    done = pl.pallas_call(
        kernel,
        out_shape=(
            jax.ShapeDtypeStruct((ROWS, WIDTH), bf16),
            jax.ShapeDtypeStruct((ROWS, HD), bf16),
        ),
        in_specs=[hbm] * 11,
        out_specs=(hbm, hbm),
        scratch_shapes=[
            pltpu.VMEM((1, NH * WIDTH), f32),
            pltpu.VMEM((3, 3, WIDTH), f32),
            pltpu.VMEM((MODES, WIDTH), f32),
            pltpu.VMEM((MODES, WIDTH), f32),
            pltpu.VMEM((1, WIDTH), f32),
            pltpu.VMEM((1, NH * WIDTH), f32),
            pltpu.VMEM((NC, 1, 2 * HD), f32),
            pltpu.VMEM((ROWS, 2 * HD), f32),
            pltpu.VMEM((NH, ROWS, WIDTH), bf16),
            pltpu.VMEM((NH, ROWS, WIDTH), bf16),
            pltpu.VMEM((NH * WIDTH, 3 * WIDTH), bf16),
            pltpu.VMEM((NH * WIDTH, 3 * HD), bf16),
            pltpu.VMEM((ROWS, 3 * WIDTH), f32),
            pltpu.VMEM((ROWS, 3 * HD), f32),
            pltpu.VMEM((ROWS, 128), f32),
            pltpu.VMEM((6, ROWS + 8 + SPAN, 128), f32),
            pltpu.VMEM((16, 3 * WIDTH), bf16),
            pltpu.VMEM((16, 3 * WIDTH), bf16),
            pltpu.VMEM((MODES, WIDTH), f32),
            pltpu.VMEM((MODES, CHUNKS, WIDTH), f32),
            pltpu.VMEM((MODES, CHUNKS, WIDTH), f32),
            pltpu.VMEM((SPAN, CHUNKS, WIDTH), f32),
            pltpu.VMEM((MODES, WIDTH), f32),
            pltpu.VMEM((2 * SPAN, CHUNKS, WIDTH), f32),
            pltpu.VMEM((SPAN, CHUNKS, WIDTH), f32),
            pltpu.VMEM((SPAN, CHUNKS, WIDTH), f32),
            pltpu.VMEM((MODES, CHUNKS, WIDTH), f32),
            pltpu.VMEM((2, ROWS + SPAN, 128), f32),
            pltpu.VMEM((MODES, WIDTH), f32),
            pltpu.VMEM((NC // 2, MODES, WIDTH), f32),
            pltpu.VMEM((MODES, WIDTH), f32),
            pltpu.VMEM((MODES, WIDTH), f32),
            pltpu.VMEM((ROWS, 2 * HD), f32),
            pltpu.VMEM((HD, ROWS), bf16),
            pltpu.VMEM((2, GROUP, 2 * HD), bf16),
            pltpu.VMEM((NC, 2, GROUP, 2 * HD), bf16),
            pltpu.VMEM((1, ROWS), f32),
            pltpu.VMEM((1, ROWS), f32),
            pltpu.VMEM((HD, ROWS), f32),
            pltpu.VMEM((ROWS, HD), bf16),
            dma((9,)),
            dma,
            dma,
            dma((6,)),
            dma((2, 8)),
            dma((2, 8, NH)),
            dma((2,)),
            dma((2,)),
            dma((NC,)),
            dma((NC,)),
            dma((NC // 2, 2)),
            dma((NC, 2)),
            dma((NC // 2, 2)),
            dma((NC // 4, 2)),
        ],
        compiler_params=pltpu.CompilerParams(
            collective_id=1, has_side_effects=True, vmem_limit_bytes=56 << 20
        ),
        name="genome",
    )(
        residual,
        hyena_gain.reshape(1, -1),
        in_weight.transpose(1, 0, 2),
        short_filter,
        decay_rate.T,
        residue.T,
        skip_gain.reshape(1, -1),
        attn_gain.reshape(1, -1),
        qkv_weight.transpose(1, 0, 2),
        far.reshape(NC, 1, -1),
        near,
    )
    return pl.pallas_call(
        write,
        out_shape=(
            jax.ShapeDtypeStruct((ROWS, WIDTH), bf16),
            jax.ShapeDtypeStruct((ROWS, HD), bf16),
        ),
        in_specs=[hbm, hbm],
        out_specs=(hbm, hbm),
        scratch_shapes=[
            pltpu.VMEM((ROWS, WIDTH), bf16),
            pltpu.VMEM((ROWS, HD), bf16),
            dma((4,)),
        ],
        compiler_params=pltpu.CompilerParams(vmem_limit_bytes=56 << 20),
        name="write",
    )(*done)


def solution(mesh):
    return jax.shard_map(
        local,
        mesh=mesh,
        in_specs=(
            P("ctx", "head"),
            P(),
            P(None, None, "head"),
            P(None, None, "head"),
            P("head", None),
            P("head", None),
            P("head"),
            P(),
            P(None, None, "head"),
        ),
        out_specs=(P("ctx", "head"), P("ctx", "head")),
        check_vma=False,
    )
```
